256 devices in a mesh: row: 16 (over x, z_lo), col: 16 (over z_hi, y, core).
Axes of the slice: x: 4, y: 4, z: 8 (z_hi: 2, z_lo: 4; z = z_hi * 4 + z_lo), core: 2. Of those that a mesh axis runs over, the one named last changes fastest.
Arguments:
- kernel_tiles: bfloat16 [16, 16, 128, 128, 128], P('row', 'col'), may hold values from -0.046875 to 0.046875
- tile_rows: int32 [16, 16, 128], P('row', 'col'), may hold values from 0 to 31
- tile_cols: int32 [16, 16, 128], P('row', 'col'), may hold values from 0 to 31, as said below
- tile_counts: int32 [16, 16], P('row', 'col'), may hold values from 32 to 128, as said below
- noise: float32 [65536], P(('row', 'col')), may hold values from 0.1 to 1
- prev_block: float32 [32, 65536], P(None, ('row', 'col')), may hold values from -6 to 6
- current_block: float32 [32, 65536], P(None, ('row', 'col')), may hold values from -6 to 6
- prev_coupling: float32 [32, 32], replicated, may hold values from -1 to 1
Outputs:
- next_block: float32 [32, 65536], P(None, ('row', 'col'))
- diag_blocks: float32 [6, 32, 32], replicated
- coupling_blocks: float32 [6, 32, 32], replicated
The draws below stay inside these ranges and needn't reach their ends.
Inputs may be any that keep to these rules, and one draw needn't show every extreme that they name: Entries of tile_counts lie from 32 to 128; some device is full. For the device at grid place (r, c), every tile_cols[r, c, s] // 2 lies from r - 1 to r + 1 (a band around the device's own block rows).
All inputs are finite; a program needn't handle non-finite values.
Results may differ from the reference program's by a relative error of at most 0.04.
Values may be sent and summed in bfloat16 or wider, within the bound.
A program may use at most 64 MiB of HBM per device.

```python
import math
import jax
import jax.numpy as jnp
from jax import lax

K = 32
BS = 128
PB = 2
TILES_DEV = 128
ITERS = 6
NPTS = 65536
NBLK = 512
N_ROW = 16
N_COL = 16


def draw_tile_counts(key, part):
    key = jax.random.fold_in(key, 7)
    first_key, second_key = jax.random.split(key)
    counts = jax.random.randint(first_key, (N_ROW * N_COL,), TILES_DEV // 4, TILES_DEV + 1)
    chosen = jax.random.randint(second_key, (), 0, N_ROW * N_COL)
    places = jnp.arange(N_ROW * N_COL, dtype=jnp.int32)
    counts = jnp.where(places == chosen, TILES_DEV, counts)
    return counts.reshape(N_ROW, N_COL).astype(jnp.int32)


def draw_tile_cols(key, part):
    key = jax.random.fold_in(key, 11)
    first_key, second_key = jax.random.split(key)
    shape = (N_ROW, N_COL, TILES_DEV)
    offset = jax.random.randint(first_key, shape, -1, 2)
    within = jax.random.randint(second_key, shape, 0, PB)
    grid_r = jnp.arange(N_ROW, dtype=jnp.int32)[:, None, None]
    group = jnp.clip(grid_r + offset, 0, N_ROW - 1)
    return (group * PB + within).astype(jnp.int32)


def place_ends(drawn, stream_key, low, top_value):
    longest = drawn.shape.index(max(drawn.shape))
    spots = []
    for shift in (0, 1):
        where = [jax.random.randint(jax.random.fold_in(stream_key, axis), (), 0, length) for axis, length in enumerate(drawn.shape)]
        where[longest] = (where[longest] + shift) % drawn.shape[longest]
        spots.append(tuple(where))
    return drawn.at[spots[0]].set(low).at[spots[1]].set(top_value)


def block_levels(key, shape, cuts, smallest, high):
    gain = 1.0
    for position, blocks in cuts:
        draws = jax.random.uniform(jax.random.fold_in(jax.random.fold_in(key, 6), position), (blocks,), jnp.float32, smallest / len(cuts), high / len(cuts))
        gain = gain * jnp.repeat(jnp.exp(draws), shape[position] // blocks).reshape((-1,) + (1,) * (len(shape) - 1 - position))
    return gain


def gaussian(rng, extent, deviation, reach, cuts=(), held_as=jnp.bfloat16):
    result = deviation * jax.random.normal(rng, extent, jnp.float32)
    if cuts:
        result = result * block_levels(rng, extent, cuts, -0.22, 0.18)
    return jnp.clip(result, -reach, reach).astype(held_as)


def setup_inputs(seed: int = 0) -> dict:
    key_list = jax.random.split(jax.random.key(seed), 9)
    kernel_tiles = gaussian(key_list[0], (N_ROW, N_COL, TILES_DEV, BS, BS), (2 * BS * TILES_DEV // PB) ** -0.5, 0.046875, ((0, 16), (1, 16)))
    tile_rows = place_ends(jax.random.randint(key_list[1], (N_ROW, N_COL, TILES_DEV), 0, N_COL * PB), jax.random.fold_in(key_list[1], 1), 0, (N_COL * PB) - 1).astype(jnp.int32)
    tile_cols = draw_tile_cols(jax.random.fold_in(key_list[8], 71), 0)
    tile_counts = draw_tile_counts(jax.random.fold_in(key_list[8], 71), 0)
    noise = jnp.clip(jnp.exp(math.log(1.0) - 2.3025851 * jax.random.uniform(key_list[4], (NPTS,), jnp.float32) ** block_levels(key_list[4], (NPTS,), ((0, 256),), -0.2, 0.2)), 0.1, 1.0)
    prev_block = gaussian(key_list[5], (K, NPTS), 1.0, 6.0, ((1, 256),), jnp.float32)
    current_block = gaussian(key_list[6], (K, NPTS), 1.0, 6.0, ((1, 256),), jnp.float32)
    prev_coupling = gaussian(key_list[7], (K, K), K ** -0.5, 1.0, (), jnp.float32)
    return dict(kernel_tiles=kernel_tiles, tile_rows=tile_rows, tile_cols=tile_cols, tile_counts=tile_counts, noise=noise, prev_block=prev_block, current_block=current_block, prev_coupling=prev_coupling)


def hdot(left, right):
    return jnp.dot(left.astype(jnp.float32), right.astype(jnp.float32), precision=lax.Precision.HIGHEST, preferred_element_type=jnp.float32)

def apply_operator(current, kernel_tiles, tile_rows, tile_cols, tile_counts, noise):
    rounded = current.astype(jnp.bfloat16)
    blocked = rounded.reshape(K, NBLK, BS)
    devices = N_ROW * N_COL
    tiles_flat = kernel_tiles.reshape(devices, TILES_DEV, BS, BS)
    rows_flat = tile_rows.reshape(devices, TILES_DEV)
    cols_flat = tile_cols.reshape(devices, TILES_DEV)
    counts_flat = tile_counts.reshape(devices)
    slots = jnp.arange(TILES_DEV, dtype=jnp.int32)

    def one_device(total, inputs):
        place, tiles, rows, cols, count = inputs
        grid_r = place // N_COL
        grid_c = place % N_COL
        row_glob = (grid_r * (N_COL * PB) + rows).astype(jnp.int32)
        col_glob = ((cols // PB * N_COL + grid_c) * PB + cols % PB).astype(jnp.int32)
        live = (slots < count).astype(jnp.float32)
        tiles_f = tiles.astype(jnp.float32)
        picked = blocked[:, col_glob, :].astype(jnp.float32)
        forward = jnp.einsum('tab,ktb->kta', tiles_f, picked, precision=lax.Precision.HIGHEST)
        forward = forward * live[None, :, None]
        total = total.at[:, row_glob, :].add(forward)
        picked_rows = blocked[:, row_glob, :].astype(jnp.float32)
        mirror = jnp.einsum('tab,kta->ktb', tiles_f, picked_rows, precision=lax.Precision.HIGHEST)
        mirror = mirror * live[None, :, None]
        total = total.at[:, col_glob, :].add(mirror)
        return (total, None)
    start = jnp.zeros((K, NBLK, BS), jnp.float32)
    places = jnp.arange(devices, dtype=jnp.int32)
    total, _ = lax.scan(one_device, start, (places, tiles_flat, rows_flat, cols_flat, counts_flat))
    return total.reshape(K, NPTS) + noise[None, :] * current

def reference(kernel_tiles, tile_rows, tile_cols, tile_counts, noise, prev_block, current_block, prev_coupling):
    previous = prev_block
    current = current_block
    coupling = prev_coupling
    diag_list = []
    lower_list = []
    for step in range(ITERS):
        image = apply_operator(current, kernel_tiles, tile_rows, tile_cols, tile_counts, noise)
        first = image - hdot(coupling, previous)
        diag = hdot(current, first.T) / NPTS
        second = first - hdot(diag.T, current)
        back = hdot(previous, second.T) / NPTS
        third = second - hdot(back.T, previous)
        gram = hdot(third, third.T) / NPTS
        lower = jnp.linalg.cholesky(gram)
        following = lax.linalg.triangular_solve(lower, third, left_side=True, lower=True)
        diag_list.append(diag)
        lower_list.append(lower)
        previous = current
        current = following
        coupling = lower.T
    return (current, jnp.stack(diag_list), jnp.stack(lower_list))
```

```python
import jax
import jax.numpy as jnp
from jax import lax
from jax.experimental import pallas as pl
from jax.experimental.pallas import tpu as pltpu
from jax.sharding import PartitionSpec as P

ITERS = 6
K = 32
BS = 128
WIDTH = 256
N_ROW = 16
N_COL = 16
SLOTS = 128
PLANE = 8
MESH_IDS = pl.DeviceIdType.MESH
F32 = jnp.float32
BF16 = jnp.bfloat16


def dot_nn(left, right):
    return lax.dot_general(
        left, right, (((1,), (0,)), ((), ())), precision=lax.Precision.HIGHEST, preferred_element_type=F32
    )


def dot_nt(left, right):
    return lax.dot_general(
        left, right, (((1,), (1,)), ((), ())), precision=lax.Precision.HIGHEST, preferred_element_type=F32
    )


def band_kernel(rows_ref, cols_ref, count_ref, tiles_hbm, band_ref, tiles, total, sems):
    parts = 4
    size = SLOTS // parts
    copies = [
        pltpu.make_async_copy(
            tiles_hbm.at[pl.ds(k * size, size)], tiles.at[pl.ds(k * size, size)], sems.at[k]
        )
        for k in range(parts)
    ]
    for copy in copies:
        copy.start()

    def clear(i, carry):
        total[i] = jnp.zeros(total.shape[1:], F32)
        return carry

    lax.fori_loop(0, 2 * N_COL, clear, 0)
    first_col = 2 * (lax.axis_index("row") - 1)
    count = count_ref[0, 0]

    def add(slot, carry):
        i = rows_ref[0, slot]
        j = cols_ref[0, slot] - first_col
        total[i, j] += tiles[slot].astype(F32)
        return carry

    for k in range(parts):
        copies[k].wait()
        lax.fori_loop(k * size, jnp.minimum((k + 1) * size, count), add, 0)

    def place(c, carry):
        for half in range(2):
            for j in range(6):
                band_ref[c, half * BS : (half + 1) * BS, j * BS : (j + 1) * BS] = total[
                    2 * c + half, j
                ].astype(BF16)
        return carry

    lax.fori_loop(0, N_COL, place, 0)


def build_band(tiles, rows, cols, count):
    smem = pl.BlockSpec(memory_space=pltpu.SMEM)
    return pl.pallas_call(
        band_kernel,
        out_shape=jax.ShapeDtypeStruct((N_COL, 2 * BS, 6 * BS), BF16),
        in_specs=[smem, smem, smem, pl.BlockSpec(memory_space=pl.ANY)],
        out_specs=pl.BlockSpec(memory_space=pltpu.VMEM),
        scratch_shapes=[
            pltpu.VMEM((SLOTS, BS, BS), BF16),
            pltpu.VMEM((2 * N_COL, 6, BS, BS), F32),
            pltpu.SemaphoreType.DMA((4,)),
        ],
        compiler_params=pltpu.CompilerParams(vmem_limit_bytes=40 * 2**20),
        name="band",
    )(rows, cols, count, tiles)


def factor(gram):
    groups = K // 8
    sub = lax.broadcasted_iota(jnp.int32, (8, K), 0)
    lane = lax.broadcasted_iota(jnp.int32, (8, K), 1)
    g = [gram[8 * b : 8 * b + 8] for b in range(groups)]
    e = [jnp.where(lane == sub + 8 * b, 1.0, 0.0).astype(F32) for b in range(groups)]
    step = 4
    for base in range(0, K, step):
        a = base // 8
        spread = [
            [
                jnp.broadcast_to(g[b][:, base + j : base + j + 1], (8, K)) if b >= a else None
                for b in range(groups)
            ]
            for j in range(step)
        ]
        for j in range(step):
            s = (base + j) % 8
            pivot = spread[j][a][s : s + 1]
            guess = lax.rsqrt(pivot)
            scale = guess * (1.5 - 0.5 * (pivot * guess) * guess)
            g_row = g[a][s : s + 1] * scale
            e_row = e[a][s : s + 1] * scale
            later = {jj: spread[jj][a][s : s + 1] * scale for jj in range(j + 1, step)}
            for b in range(a, groups):
                part = spread[j][b] * scale
                if b == a:
                    part = jnp.where(sub > s, part, 0.0)
                g[b] = g[b] - part * g_row
                e[b] = e[b] - part * e_row
                for jj in range(j + 1, step):
                    spread[jj][b] = spread[jj][b] - part * later[jj]
            g[a] = jnp.where(sub == s, g_row, g[a])
            e[a] = jnp.where(sub == s, e_row, e[a])
    upper = [jnp.where(lane >= sub + 8 * b, g[b], 0.0) for b in range(groups)]
    return jnp.concatenate(upper, axis=0), jnp.concatenate(e, axis=0)


def lanczos_kernel(
    band_hbm, noise_ref, prev_ref, cur_ref, coup_ref,
    out_ref, diag_ref, upper_ref,
    band, y, coup, xband, xrows, fsend, fown, frecv, zsend, zrecv, msend, mrecv, mir,
    hloc, h1, s2, h2, h3,
    band_sem, send_sems, recv_sems, sum_send, sum_recv,
):
    r = lax.axis_index("row")
    c = lax.axis_index("col")
    x, zl = r // 4, r % 4
    zh, p = c // PLANE, c % PLANE
    z = zh * 4 + zl
    m = x * PLANE + p
    up = (lax.rem(r + 1, N_ROW), c)
    down = (lax.rem(r + N_ROW - 1, N_ROW), c)
    over = (r, lax.rem(c + PLANE, N_COL))

    def plane_dev(pp):
        return (r, zh * PLANE + pp)

    def ring_dev(zz):
        return (x * 4 + zz % 4, (zz // 4) * PLANE + p)

    def sheet_dev(mm):
        return ((mm // PLANE) * 4 + zl, zh * PLANE + mm % PLANE)

    def put(src, dst, send, recv, dev):
        pltpu.make_async_remote_copy(
            src_ref=src, dst_ref=dst, send_sem=send, recv_sem=recv, device_id=dev, device_id_type=MESH_IDS
        ).start()

    def take(ref, sem):
        pltpu.make_async_copy(ref, ref, sem).wait()

    load = pltpu.make_async_copy(band_hbm, band, band_sem)
    load.start()

    barrier = pltpu.get_barrier_semaphore()

    def greet(dev):
        pl.semaphore_signal(barrier, inc=1, device_id=dev, device_id_type=MESH_IDS)

    def greet_ring(d, carry):
        greet(ring_dev(lax.rem(z + d, PLANE)))
        return carry

    def greet_sheet(d, carry):
        greet(sheet_dev(lax.rem(m + d, 32)))
        return carry

    greet(up)
    greet(down)
    lax.fori_loop(1, PLANE, greet_ring, 0)
    lax.fori_loop(1, 32, greet_sheet, 0)
    y[K : 2 * K] = cur_ref[...]
    y[2 * K : 3 * K] = prev_ref[...]
    y[3 * K : 4 * K] = prev_ref[...]
    coup[...] = coup_ref[...]
    pl.semaphore_wait(barrier, 2 + 7 + 31)

    def forward(pp):
        out = []
        for hi in range(2):
            rows = band.at[hi * PLANE + pp]
            acc = None
            for g in range(3):
                term = lax.dot_general(
                    xband[g], rows[:, g * WIDTH : (g + 1) * WIDTH], (((1,), (1,)), ((), ())),
                    preferred_element_type=F32,
                )
                acc = term if acc is None else acc + term
            out.append(acc)
        return out

    def forward_send(d, carry):
        pp = lax.rem(p + d, PLANE)
        part = forward(pp)
        for hi in range(2):
            fsend[d - 1, hi] = part[hi].astype(BF16)
        put(fsend.at[d - 1], frecv.at[d - 1], send_sems.at[4], recv_sems.at[4], plane_dev(pp))
        return carry

    def mirror(hi, first):
        def body(k, carry):
            acc = None
            for u in range(4):
                pp = 4 * k + u
                term = jnp.dot(xrows[hi, pp], band[hi * PLANE + pp], preferred_element_type=F32)
                acc = term if acc is None else acc + term
            if first:
                mir[...] = jnp.where(k == 0, acc, mir[...] + acc)
            else:
                mir[...] += acc
            return carry

        lax.fori_loop(0, 2, body, 0)

    def iteration(it, carry):
        parity = lax.rem(it, 2)
        rounded = y[K : 2 * K].astype(BF16)
        xband[1] = rounded
        xrows[zh, p] = rounded
        own = xband.at[1]
        put(own, xband.at[0], send_sems.at[0], recv_sems.at[0], up)
        put(own, xband.at[2], send_sems.at[0], recv_sems.at[0], down)
        put(own, xrows.at[zh, p], send_sems.at[1], recv_sems.at[1], over)

        def spread_own(d, carry):
            put(own, xrows.at[zh, p], send_sems.at[2], recv_sems.at[2], plane_dev(lax.rem(p + d, PLANE)))
            return carry

        lax.fori_loop(1, PLANE, spread_own, 0)

        @pl.when(it == 0)
        def _():
            load.wait()

        take(xband.at[pl.ds(0, 2)], recv_sems.at[0])
        lax.fori_loop(1, 5, forward_send, 0)
        take(zrecv, recv_sems.at[1])
        other = xrows.at[1 - zh, p]

        def spread_other(d, carry):
            put(
                other, xrows.at[1 - zh, p], send_sems.at[3], recv_sems.at[3],
                plane_dev(lax.rem(p + d, PLANE)),
            )
            return carry

        lax.fori_loop(1, PLANE, spread_other, 0)
        lax.fori_loop(5, PLANE, forward_send, 0)
        part = forward(p)
        for hi in range(2):
            fown[hi] = part[hi]
        seven = xrows.at[0, pl.ds(0, 7)]
        take(seven, recv_sems.at[2])
        mirror(zh, True)
        take(frecv, recv_sems.at[4])

        def total(hi):
            acc = fown[hi]
            for d in range(7):
                acc = acc + frecv[d, hi].astype(F32)
            return acc

        zsend[...] = total(1 - zh).astype(BF16)
        put(zsend, zrecv, send_sems.at[5], recv_sems.at[5], over)
        fown[zh] = total(zh)
        take(seven, recv_sems.at[3])
        take(seven, send_sems.at[3])
        mirror(1 - zh, False)
        msend[0] = mir[:, :WIDTH].astype(BF16)
        msend[1] = mir[:, 2 * WIDTH :].astype(BF16)
        put(msend.at[0], mrecv.at[0], send_sems.at[6], recv_sems.at[6], down)
        put(msend.at[1], mrecv.at[1], send_sems.at[6], recv_sems.at[6], up)
        base = fown[zh] + mir[:, WIDTH : 2 * WIDTH] + noise_ref[...] * y[K : 2 * K]
        take(zrecv, recv_sems.at[5])
        base = base + zrecv[...].astype(F32)
        take(mrecv, recv_sems.at[6])
        y[0:K] = base + mrecv[0].astype(F32) + mrecv[1].astype(F32)

        gram = dot_nt(y[0 : 3 * K], y[...])
        lane = lax.broadcasted_iota(jnp.int32, (K, 4 * K), 1)
        top = jnp.where(lane < 3 * K, gram[0:K], gram[2 * K : 3 * K])
        hloc[0:4] = top.reshape(4, 8, 4 * K)
        hloc[4:8] = gram[K : 2 * K].reshape(4, 8, 4 * K)

        def send1(d, carry):
            zz = lax.rem(z + d, PLANE)
            put(hloc.at[zz], h1.at[z], sum_send.at[0], sum_recv.at[0], ring_dev(zz))
            return carry

        lax.fori_loop(1, PLANE, send1, 0)
        h1[z] = hloc[z]
        take(h1.at[pl.ds(0, 7)], sum_recv.at[0])
        piece = jnp.sum(h1[...], axis=0)
        s2[...] = piece
        h2[parity, m] = piece

        def send2(d, carry):
            put(
                s2, h2.at[parity, m], sum_send.at[1], sum_recv.at[1 + parity],
                sheet_dev(lax.rem(m + d, 32)),
            )
            return carry

        lax.fori_loop(1, 32, send2, 0)
        take(h2.at[parity, pl.ds(0, 31)], sum_recv.at[1 + parity])
        h3[z] = jnp.sum(h2[parity], axis=0)

        def send3(d, carry):
            put(h3.at[z], h3.at[z], sum_send.at[2], sum_recv.at[3], ring_dev(lax.rem(z + d, PLANE)))
            return carry

        lax.fori_loop(1, PLANE, send3, 0)
        take(h1.at[pl.ds(0, 7)], sum_recv.at[3])
        h = h3[...].reshape(8 * PLANE, 4 * K) * (1.0 / (N_ROW * N_COL * WIDTH))

        im_im, im_q, im_p, p_p = (h[0:K, k * K : (k + 1) * K] for k in range(4))
        q_im, q_q, q_p = (h[K : 2 * K, k * K : (k + 1) * K] for k in range(3))
        b = coup[...]
        diag_t = im_q - dot_nt(b, q_p)
        back_t = im_p - dot_nn(b, p_p) - dot_nn(diag_t, q_p)
        cp = b + back_t
        third = y[0:K] - dot_nn(cp, y[2 * K : 3 * K]) - dot_nn(diag_t, y[K : 2 * K])
        t_im = im_im - dot_nn(diag_t, q_im) - dot_nt(cp, im_p)
        t_q = im_q - dot_nn(diag_t, q_q) - dot_nt(cp, q_p)
        t_p = im_p - dot_nn(diag_t, q_p) - dot_nn(cp, p_p)
        upper, inverse = factor(t_im - dot_nt(t_q, diag_t) - dot_nt(t_p, cp))
        diag_ref[it] = diag_t
        upper_ref[it] = upper
        coup[...] = upper
        old = y[K : 2 * K]
        y[2 * K : 3 * K] = old
        y[3 * K : 4 * K] = old
        y[K : 2 * K] = dot_nn(inverse, third)

        take(xband.at[pl.ds(0, 2)], send_sems.at[0])
        take(zsend, send_sems.at[1])
        take(seven, send_sems.at[2])
        take(frecv, send_sems.at[4])
        take(zsend, send_sems.at[5])
        take(msend, send_sems.at[6])
        take(h1.at[pl.ds(0, 7)], sum_send.at[0])
        take(h2.at[parity, pl.ds(0, 31)], sum_send.at[1])
        take(h1.at[pl.ds(0, 7)], sum_send.at[2])
        return carry

    lax.fori_loop(0, ITERS, iteration, 0)
    out_ref[...] = y[K : 2 * K]


def lanczos(band, noise, previous, current, coupling):
    vmem = pl.BlockSpec(memory_space=pltpu.VMEM)
    panel = (K, WIDTH)
    return pl.pallas_call(
        lanczos_kernel,
        out_shape=(
            jax.ShapeDtypeStruct(panel, F32),
            jax.ShapeDtypeStruct((ITERS, K, K), F32),
            jax.ShapeDtypeStruct((ITERS, K, K), F32),
        ),
        in_specs=[pl.BlockSpec(memory_space=pl.ANY), vmem, vmem, vmem, vmem],
        out_specs=(vmem, vmem, vmem),
        scratch_shapes=[
            pltpu.VMEM((N_COL, 2 * BS, 6 * BS), BF16),
            pltpu.VMEM((4 * K, WIDTH), F32),
            pltpu.VMEM((K, K), F32),
            pltpu.VMEM((3,) + panel, BF16),
            pltpu.VMEM((2, PLANE) + panel, BF16),
            pltpu.VMEM((7, 2) + panel, BF16),
            pltpu.VMEM((2,) + panel, F32),
            pltpu.VMEM((7, 2) + panel, BF16),
            pltpu.VMEM(panel, BF16),
            pltpu.VMEM(panel, BF16),
            pltpu.VMEM((2,) + panel, BF16),
            pltpu.VMEM((2,) + panel, BF16),
            pltpu.VMEM((K, 3 * WIDTH), F32),
            pltpu.VMEM((8, 8, 4 * K), F32),
            pltpu.VMEM((8, 8, 4 * K), F32),
            pltpu.VMEM((8, 4 * K), F32),
            pltpu.VMEM((2, 32, 8, 4 * K), F32),
            pltpu.VMEM((8, 8, 4 * K), F32),
            pltpu.SemaphoreType.DMA,
            pltpu.SemaphoreType.DMA((7,)),
            pltpu.SemaphoreType.DMA((7,)),
            pltpu.SemaphoreType.DMA((3,)),
            pltpu.SemaphoreType.DMA((4,)),
        ],
        compiler_params=pltpu.CompilerParams(
            collective_id=0, has_side_effects=True, vmem_limit_bytes=40 * 2**20
        ),
        name="lanczos",
    )(band, noise, previous, current, coupling)


def on_device(
    kernel_tiles, tile_rows, tile_cols, tile_counts, noise, prev_block, current_block, prev_coupling
):
    band = build_band(kernel_tiles[0, 0], tile_rows[0], tile_cols[0], tile_counts)
    following, diag_t, upper = lanczos(band, noise[None, :], prev_block, current_block, prev_coupling)
    return (following, jnp.swapaxes(diag_t, 1, 2), jnp.swapaxes(upper, 1, 2))


def solution(mesh):
    in_specs = (
        P("row", "col", None, None, None),
        P("row", "col", None),
        P("row", "col", None),
        P("row", "col"),
        P(("row", "col")),
        P(None, ("row", "col")),
        P(None, ("row", "col")),
        P(),
    )
    out_specs = (P(None, ("row", "col")), P(), P())
    return jax.shard_map(
        on_device, mesh=mesh, in_specs=in_specs, out_specs=out_specs, check_vma=False
    )
```

```python
import jax
import jax.numpy as jnp
from jax import lax
from jax.experimental import pallas as pl
from jax.experimental.pallas import tpu as pltpu
from jax.sharding import PartitionSpec as P

ITERS = 6
K = 32
BS = 128
WIDTH = 256
N_ROW = 16
N_COL = 16
SLOTS = 128
PLANE = 8
MESH_IDS = pl.DeviceIdType.MESH
F32 = jnp.float32
BF16 = jnp.bfloat16


def dot_nn(left, right):
    return lax.dot_general(
        left, right, (((1,), (0,)), ((), ())), precision=lax.Precision.HIGHEST, preferred_element_type=F32
    )


def dot_nt(left, right):
    return lax.dot_general(
        left, right, (((1,), (1,)), ((), ())), precision=lax.Precision.HIGHEST, preferred_element_type=F32
    )


def band_kernel(rows_ref, cols_ref, count_ref, tiles_hbm, band_ref, tiles, total, sems):
    parts = 4
    size = SLOTS // parts
    copies = [
        pltpu.make_async_copy(
            tiles_hbm.at[pl.ds(k * size, size)], tiles.at[pl.ds(k * size, size)], sems.at[k]
        )
        for k in range(parts)
    ]
    for copy in copies:
        copy.start()

    def clear(i, carry):
        total[i] = jnp.zeros(total.shape[1:], F32)
        return carry

    lax.fori_loop(0, 2 * N_COL, clear, 0)
    first_col = 2 * (lax.axis_index("row") - 1)
    count = count_ref[0, 0]

    def add(slot, carry):
        i = rows_ref[0, slot]
        j = cols_ref[0, slot] - first_col
        total[i, j] += tiles[slot].astype(F32)
        return carry

    for k in range(parts):
        copies[k].wait()
        lax.fori_loop(k * size, jnp.minimum((k + 1) * size, count), add, 0)

    def place(c, carry):
        for half in range(2):
            for j in range(6):
                band_ref[c, half * BS : (half + 1) * BS, j * BS : (j + 1) * BS] = total[
                    2 * c + half, j
                ].astype(BF16)
        return carry

    lax.fori_loop(0, N_COL, place, 0)


def build_band(tiles, rows, cols, count):
    smem = pl.BlockSpec(memory_space=pltpu.SMEM)
    return pl.pallas_call(
        band_kernel,
        out_shape=jax.ShapeDtypeStruct((N_COL, 2 * BS, 6 * BS), BF16),
        in_specs=[smem, smem, smem, pl.BlockSpec(memory_space=pl.ANY)],
        out_specs=pl.BlockSpec(memory_space=pltpu.VMEM),
        scratch_shapes=[
            pltpu.VMEM((SLOTS, BS, BS), BF16),
            pltpu.VMEM((2 * N_COL, 6, BS, BS), F32),
            pltpu.SemaphoreType.DMA((4,)),
        ],
        compiler_params=pltpu.CompilerParams(vmem_limit_bytes=40 * 2**20),
        name="band",
    )(rows, cols, count, tiles)


def factor(gram):
    groups = K // 8
    sub = lax.broadcasted_iota(jnp.int32, (8, K), 0)
    lane = lax.broadcasted_iota(jnp.int32, (8, K), 1)
    g = [gram[8 * b : 8 * b + 8] for b in range(groups)]
    e = [jnp.where(lane == sub + 8 * b, 1.0, 0.0).astype(F32) for b in range(groups)]
    step = 4
    for base in range(0, K, step):
        a = base // 8
        spread = [
            [
                jnp.broadcast_to(g[b][:, base + j : base + j + 1], (8, K)) if b >= a else None
                for b in range(groups)
            ]
            for j in range(step)
        ]
        for j in range(step):
            s = (base + j) % 8
            pivot = spread[j][a][s : s + 1]
            guess = lax.rsqrt(pivot)
            scale = guess * (1.5 - 0.5 * (pivot * guess) * guess)
            g_row = g[a][s : s + 1] * scale
            e_row = e[a][s : s + 1] * scale
            later = {jj: spread[jj][a][s : s + 1] * scale for jj in range(j + 1, step)}
            for b in range(a, groups):
                part = spread[j][b] * scale
                if b == a:
                    part = jnp.where(sub > s, part, 0.0)
                g[b] = g[b] - part * g_row
                e[b] = e[b] - part * e_row
                for jj in range(j + 1, step):
                    spread[jj][b] = spread[jj][b] - part * later[jj]
            g[a] = jnp.where(sub == s, g_row, g[a])
            e[a] = jnp.where(sub == s, e_row, e[a])
    upper = [jnp.where(lane >= sub + 8 * b, g[b], 0.0) for b in range(groups)]
    return jnp.concatenate(upper, axis=0), jnp.concatenate(e, axis=0)


def lanczos_kernel(
    band_hbm, noise_ref, prev_ref, cur_ref, coup_ref,
    out_ref, diag_ref, upper_ref,
    band, ty, coup, xband, xrows, facc, fsend, fown, frecv, zsend, zrecv, msend, mrecv, mir,
    hloc, h1, s2, h2, h3,
    band_sem, send_sems, recv_sems, sum_send, sum_recv,
):
    r = lax.axis_index("row")
    c = lax.axis_index("col")
    x, zl = r // 4, r % 4
    zh, p = c // PLANE, c % PLANE
    z = zh * 4 + zl
    m = x * 8 + z
    up = (lax.rem(r + 1, N_ROW), c)
    down = (lax.rem(r + N_ROW - 1, N_ROW), c)
    over = (r, lax.rem(c + PLANE, N_COL))

    def plane_dev(pp):
        return (r, zh * PLANE + pp)

    def sheet_dev(d):
        xx = lax.rem(x + 2 + d // 8, 4)
        zz = lax.rem(z + 4 + d % 8, 8)
        return (xx * 4 + zz % 4, (zz // 4) * PLANE + p)

    def on_plane(body):
        lax.fori_loop(1, PLANE, lambda d, carry: (body(d, lax.rem(p + d, PLANE)), carry)[1], 0)

    def on_sheet(body):
        lax.fori_loop(0, 20, lambda d, carry: (body(sheet_dev(d)), carry)[1], 0)
        lax.fori_loop(21, 32, lambda d, carry: (body(sheet_dev(d)), carry)[1], 0)

    def put(src, dst, send, recv, dev):
        pltpu.make_async_remote_copy(
            src_ref=src, dst_ref=dst, send_sem=send, recv_sem=recv, device_id=dev, device_id_type=MESH_IDS
        ).start()

    def take(ref, sem):
        pltpu.make_async_copy(ref, ref, sem).wait()

    load = pltpu.make_async_copy(band_hbm, band, band_sem)
    load.start()

    barrier = pltpu.get_barrier_semaphore()

    def greet(dev):
        pl.semaphore_signal(barrier, inc=1, device_id=dev, device_id_type=MESH_IDS)

    on_sheet(greet)
    on_plane(lambda d, pp: greet(plane_dev(pp)))
    ty[...] = jnp.zeros_like(ty)
    ty[K : 2 * K, :WIDTH] = cur_ref[...]
    ty[2 * K :, :WIDTH] = prev_ref[...]
    coup[...] = coup_ref[...]
    pl.semaphore_wait(barrier, 7 + 31)


    def spread(n, par):
        own = xband.at[par, 1, pl.ds(0, n)]
        put(own, xband.at[par, 0, pl.ds(0, n)], send_sems.at[0], recv_sems.at[par, 0], up)
        put(own, xband.at[par, 2, pl.ds(0, n)], send_sems.at[0], recv_sems.at[par, 0], down)
        place = xrows.at[par, zh, p, pl.ds(0, n)]
        put(own, place, send_sems.at[1], recv_sems.at[par, 1], over)
        on_plane(lambda d, pp: put(own, place, send_sems.at[2], recv_sems.at[par, 2], plane_dev(pp)))
        xrows[par, zh, p, :n] = xband[par, 1, :n]

    def own_forward(n, par):
        def body(k, carry):
            for u in range(4):
                facc[4 * k + u, :n] = lax.dot_general(
                    xband[par, 1, :n], band[4 * k + u, :, WIDTH : 2 * WIDTH], (((1,), (1,)), ((), ())),
                    preferred_element_type=F32,
                )
            return carry

        lax.fori_loop(0, 4, body, 0)

    def pass_on(n, par):
        take(xband.at[par, pl.ds(0, 2), pl.ds(0, n)], recv_sems.at[par, 0])
        take(zrecv.at[par, pl.ds(0, n)], recv_sems.at[par, 1])
        other = xrows.at[par, 1 - zh, p, pl.ds(0, n)]
        on_plane(lambda d, pp: put(other, other, send_sems.at[3], recv_sems.at[par, 3], plane_dev(pp)))

    def forward(n, par, half):
        hi = 1 - zh if half == 0 else zh

        def product(pp):
            acc = facc[hi * PLANE + pp, :n]
            for g in (0, 2):
                acc = acc + lax.dot_general(
                    xband[par, g, :n], band[hi * PLANE + pp, :, g * WIDTH : (g + 1) * WIDTH],
                    (((1,), (1,)), ((), ())), preferred_element_type=F32,
                )
            return acc

        def send(d):
            put(
                fsend.at[half, d - 1, pl.ds(0, n)], frecv.at[par, half, d - 1, pl.ds(0, n)],
                send_sems.at[4 + half], recv_sems.at[par, 4 + half], plane_dev(lax.rem(p + d, PLANE)),
            )

        def body(k, carry):
            d = 2 * k + 1
            first = product(lax.rem(p + d, PLANE))
            second = product(lax.rem(p + d + 1, PLANE))
            fsend[half, d - 1, :n] = first.astype(BF16)
            fsend[half, d, :n] = second.astype(BF16)
            send(d)
            send(d + 1)
            return carry

        lax.fori_loop(0, 3, body, 0)
        first = product(lax.rem(p + 7, PLANE))
        second = product(p)
        fsend[half, 6, :n] = first.astype(BF16)
        fown[half, :n] = second
        send(7)

    def seven(n):
        return xrows.at[0, 0, pl.ds(0, 7), pl.ds(0, n)]

    def mirror(n, par, hi, first):
        def body(k, carry):
            acc = None
            for u in range(4):
                pp = 4 * k + u
                term = jnp.dot(
                    xrows[par, hi, pp, :n], band[hi * PLANE + pp], preferred_element_type=F32
                )
                acc = term if acc is None else acc + term
            if first:
                mir[:n] = jnp.where(k == 0, acc, mir[:n] + acc)
            else:
                mir[:n] += acc
            return carry

        lax.fori_loop(0, 2, body, 0)

    def mirror_near(n, par):
        take(seven(n), recv_sems.at[par, 2])
        mirror(n, par, zh, True)

    def mirror_far(n, par):
        take(seven(n), recv_sems.at[par, 3])
        mirror(n, par, 1 - zh, False)
        msend[0, :n] = mir[:n, :WIDTH].astype(BF16)
        msend[1, :n] = mir[:n, 2 * WIDTH :].astype(BF16)
        for g, dev in ((0, down), (1, up)):
            put(
                msend.at[g, pl.ds(0, n)], mrecv.at[par, g, pl.ds(0, n)],
                send_sems.at[6], recv_sems.at[par, 6], dev,
            )

    def total(n, par, half):
        take(frecv.at[par, half, :, pl.ds(0, n)], recv_sems.at[par, 4 + half])
        acc = fown[half, :n]
        for d in range(7):
            acc = acc + frecv[par, half, d, :n].astype(F32)
        return acc

    def send_over(n, par):
        zsend[:n] = total(n, par, 0).astype(BF16)
        put(
            zsend.at[pl.ds(0, n)], zrecv.at[par, pl.ds(0, n)], send_sems.at[7], recv_sems.at[par, 7], over
        )

    def gather_image(n, par, vectors):
        acc = total(n, par, 1) + mir[:n, WIDTH : 2 * WIDTH] + noise_ref[...] * vectors
        take(mrecv.at[par, :, pl.ds(0, n)], recv_sems.at[par, 6])
        acc = acc + mrecv[par, 0, :n].astype(F32) + mrecv[par, 1, :n].astype(F32)
        take(zrecv.at[par, pl.ds(0, n)], recv_sems.at[par, 7])
        return acc + zrecv[par, :n].astype(F32)

    def all_left(n):
        one = zsend.at[pl.ds(0, n)]
        take(msend.at[:, pl.ds(0, n)], send_sems.at[0])
        take(one, send_sems.at[1])
        take(seven(n), send_sems.at[2])
        take(seven(n), send_sems.at[3])
        take(seven(n), send_sems.at[4])
        take(seven(n), send_sems.at[5])
        take(msend.at[:, pl.ds(0, n)], send_sems.at[6])
        take(one, send_sems.at[7])

    xband[1, 1, :K] = cur_ref[...].astype(BF16)
    xband[1, 1, K:] = prev_ref[...].astype(BF16)
    spread(2 * K, 1)
    load.wait()
    own_forward(2 * K, 1)
    pass_on(2 * K, 1)
    forward(2 * K, 1, 0)
    forward(2 * K, 1, 1)
    mirror_near(2 * K, 1)
    mirror_far(2 * K, 1)
    send_over(2 * K, 1)
    images = gather_image(2 * K, 1, ty[K:, :WIDTH])
    ty[K:, WIDTH:] = images
    xband[0, 1, :K] = images[:K].astype(BF16)
    all_left(2 * K)

    def iteration(it, carry):
        par = lax.rem(it, 2)
        more = it < ITERS - 1

        @pl.when(more)
        def _():
            spread(K, par)

        ty[:K, :WIDTH] = xband[par, 1, :K].astype(F32)
        y = ty[:, :WIDTH]
        gram = dot_nt(y, jnp.concatenate([y, y[2 * K :]], axis=0))
        lane = lax.broadcasted_iota(jnp.int32, (K, 4 * K), 1)
        top = jnp.where(lane < 3 * K, gram[0:K], gram[2 * K : 3 * K])
        hloc[0:4] = top.reshape(4, 8, 4 * K)
        hloc[4:8] = gram[K : 2 * K].reshape(4, 8, 4 * K)
        on_plane(lambda d, pp: put(hloc.at[pp], h1.at[p], sum_send.at[0], sum_recv.at[0], plane_dev(pp)))
        h1[p] = hloc[p]

        @pl.when(more)
        def _():
            own_forward(K, par)

        take(h1.at[pl.ds(0, 7)], sum_recv.at[0])
        piece = jnp.sum(h1[...], axis=0)
        s2[...] = piece
        h2[par, m] = piece
        on_sheet(lambda dev: put(s2, h2.at[par, m], sum_send.at[1], sum_recv.at[1 + par], dev))

        @pl.when(more)
        def _():
            pass_on(K, par)
            forward(K, par, 0)
            forward(K, par, 1)
            mirror_near(K, par)
            mirror_far(K, par)
            send_over(K, par)

        take(h2.at[par, pl.ds(0, 31)], sum_recv.at[1 + par])
        h3[p] = jnp.sum(h2[par], axis=0)
        on_plane(lambda d, pp: put(h3.at[p], h3.at[p], sum_send.at[2], sum_recv.at[3], plane_dev(pp)))

        @pl.when(more)
        def _():
            ty[:K, WIDTH:] = gather_image(K, par, ty[:K, :WIDTH])

        take(h1.at[pl.ds(0, 7)], sum_recv.at[3])
        h = h3[...].reshape(8 * PLANE, 4 * K) * (1.0 / (N_ROW * N_COL * WIDTH))

        im_im, im_q, im_p, p_p = (h[0:K, k * K : (k + 1) * K] for k in range(4))
        q_im, q_q, q_p = (h[K : 2 * K, k * K : (k + 1) * K] for k in range(3))
        b = coup[...]
        diag_t = im_q - dot_nt(b, q_p)
        cp = b + (im_p - dot_nn(b, p_p) - dot_nn(diag_t, q_p))
        third = ty[:K] - dot_nn(cp, ty[2 * K :]) - dot_nn(diag_t, ty[K : 2 * K])
        t_im = im_im - dot_nn(diag_t, q_im) - dot_nt(cp, im_p)
        t_q = im_q - dot_nn(diag_t, q_q) - dot_nt(cp, q_p)
        t_p = im_p - dot_nn(diag_t, q_p) - dot_nn(cp, p_p)
        upper, inverse = factor(t_im - dot_nt(t_q, diag_t) - dot_nt(t_p, cp))
        following = dot_nn(inverse, third)
        diag_ref[it] = diag_t
        upper_ref[it] = upper
        coup[...] = upper
        ty[2 * K :] = ty[K : 2 * K]
        ty[K : 2 * K] = following
        xband[1 - par, 1, :K] = following[:, WIDTH:].astype(BF16)

        @pl.when(more)
        def _():
            all_left(K)

        take(h1.at[pl.ds(0, 7)], sum_send.at[0])
        take(h2.at[par, pl.ds(0, 31)], sum_send.at[1])
        take(h1.at[pl.ds(0, 7)], sum_send.at[2])
        return carry

    lax.fori_loop(0, ITERS, iteration, 0)
    out_ref[...] = ty[K : 2 * K, :WIDTH]


def lanczos(band, noise, previous, current, coupling):
    vmem = pl.BlockSpec(memory_space=pltpu.VMEM)
    panel = (K, WIDTH)
    two = (2 * K, WIDTH)
    piece = (8, 4 * K)
    return pl.pallas_call(
        lanczos_kernel,
        out_shape=(
            jax.ShapeDtypeStruct(panel, F32),
            jax.ShapeDtypeStruct((ITERS, K, K), F32),
            jax.ShapeDtypeStruct((ITERS, K, K), F32),
        ),
        in_specs=[pl.BlockSpec(memory_space=pl.ANY), vmem, vmem, vmem, vmem],
        out_specs=(vmem, vmem, vmem),
        scratch_shapes=[
            pltpu.VMEM((N_COL, 2 * BS, 6 * BS), BF16),
            pltpu.VMEM((3 * K, 2 * WIDTH), F32),
            pltpu.VMEM((K, K), F32),
            pltpu.VMEM((2, 3) + two, BF16),
            pltpu.VMEM((2, 2, PLANE) + two, BF16),
            pltpu.VMEM((N_COL,) + two, F32),
            pltpu.VMEM((2, 7) + two, BF16),
            pltpu.VMEM((2,) + two, F32),
            pltpu.VMEM((2, 2, 7) + two, BF16),
            pltpu.VMEM(two, BF16),
            pltpu.VMEM((2,) + two, BF16),
            pltpu.VMEM((2,) + two, BF16),
            pltpu.VMEM((2, 2) + two, BF16),
            pltpu.VMEM((2 * K, 3 * WIDTH), F32),
            pltpu.VMEM((8,) + piece, F32),
            pltpu.VMEM((8,) + piece, F32),
            pltpu.VMEM(piece, F32),
            pltpu.VMEM((2, 32) + piece, F32),
            pltpu.VMEM((8,) + piece, F32),
            pltpu.SemaphoreType.DMA,
            pltpu.SemaphoreType.DMA((8,)),
            pltpu.SemaphoreType.DMA((2, 8)),
            pltpu.SemaphoreType.DMA((3,)),
            pltpu.SemaphoreType.DMA((4,)),
        ],
        compiler_params=pltpu.CompilerParams(
            collective_id=0, has_side_effects=True, vmem_limit_bytes=40 * 2**20
        ),
        name="lanczos",
    )(band, noise, previous, current, coupling)


def on_device(
    kernel_tiles, tile_rows, tile_cols, tile_counts, noise, prev_block, current_block, prev_coupling
):
    band = build_band(kernel_tiles[0, 0], tile_rows[0], tile_cols[0], tile_counts)
    following, diag_t, upper = lanczos(band, noise[None, :], prev_block, current_block, prev_coupling)
    return (following, jnp.swapaxes(diag_t, 1, 2), jnp.swapaxes(upper, 1, 2))


def solution(mesh):
    in_specs = (
        P("row", "col", None, None, None),
        P("row", "col", None),
        P("row", "col", None),
        P("row", "col"),
        P(("row", "col")),
        P(None, ("row", "col")),
        P(None, ("row", "col")),
        P(),
    )
    out_specs = (P(None, ("row", "col")), P(), P())
    return jax.shard_map(
        on_device, mesh=mesh, in_specs=in_specs, out_specs=out_specs, check_vma=False
    )
```

```python
import jax
import jax.numpy as jnp
from jax import lax
from jax.experimental import pallas as pl
from jax.experimental.pallas import tpu as pltpu
from jax.sharding import PartitionSpec as P

ITERS = 6
K = 32
BS = 128
WIDTH = 256
N_ROW = 16
N_COL = 16
SLOTS = 128
PLANE = 8
MESH_IDS = pl.DeviceIdType.MESH
F32 = jnp.float32
BF16 = jnp.bfloat16


def dot_nn(left, right):
    return lax.dot_general(
        left, right, (((1,), (0,)), ((), ())), precision=lax.Precision.HIGHEST, preferred_element_type=F32
    )


def dot_nt(left, right):
    return lax.dot_general(
        left, right, (((1,), (1,)), ((), ())), precision=lax.Precision.HIGHEST, preferred_element_type=F32
    )


def band_kernel(rows_ref, cols_ref, count_ref, tiles_hbm, band_ref, tiles, total, sems):
    parts = 4
    size = SLOTS // parts
    copies = [
        pltpu.make_async_copy(
            tiles_hbm.at[pl.ds(k * size, size)], tiles.at[pl.ds(k * size, size)], sems.at[k]
        )
        for k in range(parts)
    ]
    for copy in copies:
        copy.start()

    def clear(i, carry):
        total[i] = jnp.zeros(total.shape[1:], F32)
        return carry

    lax.fori_loop(0, 2 * N_COL, clear, 0)
    first_col = 2 * (lax.axis_index("row") - 1)
    count = count_ref[0, 0]

    def add(slot, carry):
        i = rows_ref[0, slot]
        j = cols_ref[0, slot] - first_col
        total[i, j] += tiles[slot].astype(F32)
        return carry

    for k in range(parts):
        copies[k].wait()
        lax.fori_loop(k * size, jnp.minimum((k + 1) * size, count), add, 0)

    def place(c, carry):
        for half in range(2):
            for j in range(6):
                band_ref[c, half * BS : (half + 1) * BS, j * BS : (j + 1) * BS] = total[
                    2 * c + half, j
                ].astype(BF16)
        return carry

    lax.fori_loop(0, N_COL, place, 0)


def build_band(tiles, rows, cols, count):
    smem = pl.BlockSpec(memory_space=pltpu.SMEM)
    return pl.pallas_call(
        band_kernel,
        out_shape=jax.ShapeDtypeStruct((N_COL, 2 * BS, 6 * BS), BF16),
        in_specs=[smem, smem, smem, pl.BlockSpec(memory_space=pl.ANY)],
        out_specs=pl.BlockSpec(memory_space=pltpu.VMEM),
        scratch_shapes=[
            pltpu.VMEM((SLOTS, BS, BS), BF16),
            pltpu.VMEM((2 * N_COL, 6, BS, BS), F32),
            pltpu.SemaphoreType.DMA((4,)),
        ],
        compiler_params=pltpu.CompilerParams(vmem_limit_bytes=40 * 2**20),
        name="band",
    )(rows, cols, count, tiles)


def factor(gram):
    groups = K // 8
    sub = lax.broadcasted_iota(jnp.int32, (8, K), 0)
    lane = lax.broadcasted_iota(jnp.int32, (8, K), 1)
    g = [gram[8 * b : 8 * b + 8] for b in range(groups)]
    e = [jnp.where(lane == sub + 8 * b, 1.0, 0.0).astype(F32) for b in range(groups)]
    step = 4
    for base in range(0, K, step):
        a = base // 8
        spread = [
            [
                jnp.broadcast_to(g[b][:, base + j : base + j + 1], (8, K)) if b >= a else None
                for b in range(groups)
            ]
            for j in range(step)
        ]
        for j in range(step):
            s = (base + j) % 8
            pivot = spread[j][a][s : s + 1]
            guess = lax.rsqrt(pivot)
            scale = guess * (1.5 - 0.5 * (pivot * guess) * guess)
            g_row = g[a][s : s + 1] * scale
            e_row = e[a][s : s + 1] * scale
            later = {jj: spread[jj][a][s : s + 1] * scale for jj in range(j + 1, step)}
            for b in range(a, groups):
                part = spread[j][b] * scale
                if b == a:
                    part = jnp.where(sub > s, part, 0.0)
                g[b] = g[b] - part * g_row
                e[b] = e[b] - part * e_row
                for jj in range(j + 1, step):
                    spread[jj][b] = spread[jj][b] - part * later[jj]
            g[a] = jnp.where(sub == s, g_row, g[a])
            e[a] = jnp.where(sub == s, e_row, e[a])
    upper = [jnp.where(lane >= sub + 8 * b, g[b], 0.0) for b in range(groups)]
    return jnp.concatenate(upper, axis=0), jnp.concatenate(e, axis=0)


def lanczos_kernel(
    band, noise_ref, prev_ref, cur_ref, coup_ref,
    out_ref, diag_ref, upper_ref,
    ty, known, xband, xrows, facc, fsend, fown, frecv, zsend, zrecv, msend, mrecv, mir,
    hloc, h1, s2, h2, h3,
    send_sems, recv_sems, sum_send, sum_recv,
):
    r = lax.axis_index("row")
    c = lax.axis_index("col")
    x, zl = r // 4, r % 4
    zh, p = c // PLANE, c % PLANE
    z = zh * 4 + zl
    m = x * 8 + z
    up = (lax.rem(r + 1, N_ROW), c)
    down = (lax.rem(r + N_ROW - 1, N_ROW), c)
    over = (r, lax.rem(c + PLANE, N_COL))

    def plane_dev(pp):
        return (r, zh * PLANE + pp)

    def sheet_dev(d):
        xx = lax.rem(x + 2 + d // 8, 4)
        zz = lax.rem(z + 4 + d % 8, 8)
        return (xx * 4 + zz % 4, (zz // 4) * PLANE + p)

    def on_plane(body):
        lax.fori_loop(1, PLANE, lambda d, carry: (body(d, lax.rem(p + d, PLANE)), carry)[1], 0)

    def on_sheet(body):
        lax.fori_loop(0, 20, lambda d, carry: (body(sheet_dev(d)), carry)[1], 0)
        lax.fori_loop(21, 32, lambda d, carry: (body(sheet_dev(d)), carry)[1], 0)

    def put(src, dst, send, recv, dev):
        pltpu.make_async_remote_copy(
            src_ref=src, dst_ref=dst, send_sem=send, recv_sem=recv, device_id=dev, device_id_type=MESH_IDS
        ).start()

    def take(ref, sem):
        pltpu.make_async_copy(ref, ref, sem).wait()

    barrier = pltpu.get_barrier_semaphore()

    def greet(dev):
        pl.semaphore_signal(barrier, inc=1, device_id=dev, device_id_type=MESH_IDS)

    on_sheet(greet)
    on_plane(lambda d, pp: greet(plane_dev(pp)))
    ty[...] = jnp.zeros_like(ty)
    ty[K : 2 * K, :WIDTH] = cur_ref[...]
    ty[2 * K :, :WIDTH] = prev_ref[...]
    known[0] = coup_ref[...]
    pl.semaphore_wait(barrier, 7 + 31)


    def spread(n, par):
        own = xband.at[par, 1, pl.ds(0, n)]
        put(own, xband.at[par, 0, pl.ds(0, n)], send_sems.at[0], recv_sems.at[par, 0], up)
        put(own, xband.at[par, 2, pl.ds(0, n)], send_sems.at[0], recv_sems.at[par, 0], down)
        place = xrows.at[par, zh, p, pl.ds(0, n)]
        put(own, place, send_sems.at[1], recv_sems.at[par, 1], over)
        on_plane(lambda d, pp: put(own, place, send_sems.at[2], recv_sems.at[par, 2], plane_dev(pp)))
        xrows[par, zh, p, :n] = xband[par, 1, :n]

    def own_forward(n, par):
        def body(k, carry):
            for u in range(4):
                facc[4 * k + u, :n] = lax.dot_general(
                    xband[par, 1, :n], band[4 * k + u, :, WIDTH : 2 * WIDTH], (((1,), (1,)), ((), ())),
                    preferred_element_type=F32,
                )
            return carry

        lax.fori_loop(0, 4, body, 0)

    def pass_on(n, par):
        take(xband.at[par, pl.ds(0, 2), pl.ds(0, n)], recv_sems.at[par, 0])
        take(zrecv.at[par, pl.ds(0, n)], recv_sems.at[par, 1])
        other = xrows.at[par, 1 - zh, p, pl.ds(0, n)]
        on_plane(lambda d, pp: put(other, other, send_sems.at[3], recv_sems.at[par, 3], plane_dev(pp)))

    def forward(n, par, half):
        hi = 1 - zh if half == 0 else zh

        def product(pp):
            acc = facc[hi * PLANE + pp, :n]
            for g in (0, 2):
                acc = acc + lax.dot_general(
                    xband[par, g, :n], band[hi * PLANE + pp, :, g * WIDTH : (g + 1) * WIDTH],
                    (((1,), (1,)), ((), ())), preferred_element_type=F32,
                )
            return acc

        def send(d):
            put(
                fsend.at[half, d - 1, pl.ds(0, n)], frecv.at[par, half, d - 1, pl.ds(0, n)],
                send_sems.at[4 + half], recv_sems.at[par, 4 + half], plane_dev(lax.rem(p + d, PLANE)),
            )

        def body(k, carry):
            d = 2 * k + 1
            first = product(lax.rem(p + d, PLANE))
            second = product(lax.rem(p + d + 1, PLANE))
            fsend[half, d - 1, :n] = first.astype(BF16)
            fsend[half, d, :n] = second.astype(BF16)
            send(d)
            send(d + 1)
            return carry

        lax.fori_loop(0, 3, body, 0)
        first = product(lax.rem(p + 7, PLANE))
        second = product(p)
        fsend[half, 6, :n] = first.astype(BF16)
        fown[half, :n] = second
        send(7)

    def seven(n):
        return xrows.at[0, 0, pl.ds(0, 7), pl.ds(0, n)]

    def mirror(n, par, hi, first):
        def body(k, carry):
            acc = None
            for u in range(4):
                pp = 4 * k + u
                term = jnp.dot(
                    xrows[par, hi, pp, :n], band[hi * PLANE + pp], preferred_element_type=F32
                )
                acc = term if acc is None else acc + term
            if first:
                mir[:n] = jnp.where(k == 0, acc, mir[:n] + acc)
            else:
                mir[:n] += acc
            return carry

        lax.fori_loop(0, 2, body, 0)

    def mirror_near(n, par):
        take(seven(n), recv_sems.at[par, 2])
        mirror(n, par, zh, True)

    def mirror_far(n, par):
        take(seven(n), recv_sems.at[par, 3])
        mirror(n, par, 1 - zh, False)
        msend[0, :n] = mir[:n, :WIDTH].astype(BF16)
        msend[1, :n] = mir[:n, 2 * WIDTH :].astype(BF16)
        for g, dev in ((0, down), (1, up)):
            put(
                msend.at[g, pl.ds(0, n)], mrecv.at[par, g, pl.ds(0, n)],
                send_sems.at[6], recv_sems.at[par, 6], dev,
            )

    def total(n, par, half):
        take(frecv.at[par, half, :, pl.ds(0, n)], recv_sems.at[par, 4 + half])
        acc = fown[half, :n]
        for d in range(7):
            acc = acc + frecv[par, half, d, :n].astype(F32)
        return acc

    def send_over(n, par):
        zsend[:n] = total(n, par, 0).astype(BF16)
        put(
            zsend.at[pl.ds(0, n)], zrecv.at[par, pl.ds(0, n)], send_sems.at[7], recv_sems.at[par, 7], over
        )

    def gather_image(n, par, vectors):
        acc = total(n, par, 1) + mir[:n, WIDTH : 2 * WIDTH] + noise_ref[...] * vectors
        take(mrecv.at[par, :, pl.ds(0, n)], recv_sems.at[par, 6])
        acc = acc + mrecv[par, 0, :n].astype(F32) + mrecv[par, 1, :n].astype(F32)
        take(zrecv.at[par, pl.ds(0, n)], recv_sems.at[par, 7])
        return acc + zrecv[par, :n].astype(F32)

    def all_left(n):
        one = zsend.at[pl.ds(0, n)]
        take(msend.at[:, pl.ds(0, n)], send_sems.at[0])
        take(one, send_sems.at[1])
        take(seven(n), send_sems.at[2])
        take(seven(n), send_sems.at[3])
        take(seven(n), send_sems.at[4])
        take(seven(n), send_sems.at[5])
        take(msend.at[:, pl.ds(0, n)], send_sems.at[6])
        take(one, send_sems.at[7])


    def sum_first(part):
        for k in range(PLANE):
            hloc[k] = part[4 * k : 4 * k + 4]
        on_plane(lambda d, pp: put(hloc.at[pp], h1.at[p], sum_send.at[0], sum_recv.at[0], plane_dev(pp)))
        h1[p] = hloc[p]

    def sum_second(par):
        take(h1.at[pl.ds(0, 7)], sum_recv.at[0])
        piece = jnp.sum(h1[...], axis=0)
        s2[...] = piece
        h2[par, m] = piece
        on_sheet(lambda dev: put(s2, h2.at[par, m], sum_send.at[1], sum_recv.at[1 + par], dev))

    def sum_third(par):
        take(h2.at[par, pl.ds(0, 31)], sum_recv.at[1 + par])
        h3[p] = jnp.sum(h2[par], axis=0)
        on_plane(lambda d, pp: put(h3.at[p], h3.at[p], sum_send.at[2], sum_recv.at[3], plane_dev(pp)))

    def sum_result():
        take(h1.at[pl.ds(0, 7)], sum_recv.at[3])
        h = jnp.concatenate([h3[k] for k in range(PLANE)], axis=0)
        h = h * (1.0 / (N_ROW * N_COL * WIDTH))
        return [h[:, k * K : (k + 1) * K] for k in range(3)]

    def sum_left(par):
        take(h1.at[pl.ds(0, 7)], sum_send.at[0])
        take(h2.at[par, pl.ds(0, 31)], sum_send.at[1])
        take(h1.at[pl.ds(0, 7)], sum_send.at[2])

    lane = lax.broadcasted_iota(jnp.int32, (K, 4 * K), 1)

    xband[1, 1, :K] = cur_ref[...].astype(BF16)
    xband[1, 1, K:] = prev_ref[...].astype(BF16)
    spread(2 * K, 1)
    q_and_p = ty[K:, :WIDTH]
    both = dot_nt(q_and_p, jnp.concatenate([q_and_p, ty[2 * K :, :WIDTH], ty[2 * K :, :WIDTH]], axis=0))
    sum_first(jnp.where(lane < 2 * K, both[:K], both[K:]))
    own_forward(2 * K, 1)
    sum_second(1)
    pass_on(2 * K, 1)
    forward(2 * K, 1, 0)
    forward(2 * K, 1, 1)
    mirror_near(2 * K, 1)
    mirror_far(2 * K, 1)
    send_over(2 * K, 1)
    sum_third(1)
    images = gather_image(2 * K, 1, ty[K:, :WIDTH])
    ty[K:, WIDTH:] = images
    xband[0, 1, :K] = images[:K].astype(BF16)
    all_left(2 * K)
    spread(K, 0)
    for k, value in enumerate(sum_result()):
        known[1 + k] = value
    sum_left(1)

    def iteration(it, carry):
        par = lax.rem(it, 2)
        more = it < ITERS - 1

        ty[:K, :WIDTH] = xband[par, 1, :K].astype(F32)
        y = ty[:, :WIDTH]
        sum_first(dot_nt(y[:K], jnp.concatenate([y, y[2 * K :]], axis=0)))
        b, q_q, q_p, p_p = (known[k] for k in range(4))
        b_qp = dot_nt(b, q_p)
        b_pp = b - dot_nn(b, p_p)

        @pl.when(more)
        def _():
            own_forward(K, par)

        sum_second(par)

        @pl.when(more)
        def _():
            pass_on(K, par)
            forward(K, par, 0)
            forward(K, par, 1)
            mirror_near(K, par)
            mirror_far(K, par)
            send_over(K, par)

        sum_third(par)
        im_im, im_q, im_p = sum_result()
        diag_t = im_q - b_qp
        cp = im_p + b_pp - dot_nn(diag_t, q_p)
        t_im = im_im - dot_nt(diag_t, im_q) - dot_nt(cp, im_p)
        t_q = im_q - dot_nn(diag_t, q_q) - dot_nt(cp, q_p)
        t_p = im_p - dot_nn(diag_t, q_p) - dot_nn(cp, p_p)
        gram = t_im - dot_nt(t_q, diag_t) - dot_nt(t_p, cp)
        rest = dot_nn(cp, ty[2 * K :]) + dot_nn(diag_t, ty[K : 2 * K])
        upper, inverse = factor(gram)

        @pl.when(more)
        def _():
            ty[:K, WIDTH:] = gather_image(K, par, ty[:K, :WIDTH])

        following = dot_nn(inverse, ty[:K] - rest)
        xband[1 - par, 1, :K] = following[:, WIDTH:].astype(BF16)

        @pl.when(more)
        def _():
            all_left(K)

        sum_left(par)

        @pl.when(it < ITERS - 2)
        def _():
            spread(K, 1 - par)

        ty[2 * K :] = ty[K : 2 * K]
        ty[K : 2 * K] = following
        diag_ref[it] = diag_t
        upper_ref[it] = upper
        known[0] = upper
        known[1] = dot_nt(dot_nn(inverse, gram), inverse)
        known[2] = dot_nn(inverse, t_q)
        known[3] = q_q
        return carry

    lax.fori_loop(0, ITERS, iteration, 0)
    out_ref[...] = ty[K : 2 * K, :WIDTH]


def lanczos(band, noise, previous, current, coupling):
    vmem = pl.BlockSpec(memory_space=pltpu.VMEM)
    panel = (K, WIDTH)
    two = (2 * K, WIDTH)
    piece = (4, 4 * K)
    return pl.pallas_call(
        lanczos_kernel,
        out_shape=(
            jax.ShapeDtypeStruct(panel, F32),
            jax.ShapeDtypeStruct((ITERS, K, K), F32),
            jax.ShapeDtypeStruct((ITERS, K, K), F32),
        ),
        in_specs=[vmem, vmem, vmem, vmem, vmem],
        out_specs=(vmem, vmem, vmem),
        scratch_shapes=[
            pltpu.VMEM((3 * K, 2 * WIDTH), F32),
            pltpu.VMEM((4, K, K), F32),
            pltpu.VMEM((2, 3) + two, BF16),
            pltpu.VMEM((2, 2, PLANE) + two, BF16),
            pltpu.VMEM((N_COL,) + two, F32),
            pltpu.VMEM((2, 7) + two, BF16),
            pltpu.VMEM((2,) + two, F32),
            pltpu.VMEM((2, 2, 7) + two, BF16),
            pltpu.VMEM(two, BF16),
            pltpu.VMEM((2,) + two, BF16),
            pltpu.VMEM((2,) + two, BF16),
            pltpu.VMEM((2, 2) + two, BF16),
            pltpu.VMEM((2 * K, 3 * WIDTH), F32),
            pltpu.VMEM((8,) + piece, F32),
            pltpu.VMEM((8,) + piece, F32),
            pltpu.VMEM(piece, F32),
            pltpu.VMEM((2, 32) + piece, F32),
            pltpu.VMEM((8,) + piece, F32),
            pltpu.SemaphoreType.DMA((8,)),
            pltpu.SemaphoreType.DMA((2, 8)),
            pltpu.SemaphoreType.DMA((3,)),
            pltpu.SemaphoreType.DMA((4,)),
        ],
        compiler_params=pltpu.CompilerParams(
            collective_id=0, has_side_effects=True, vmem_limit_bytes=40 * 2**20
        ),
        name="lanczos",
    )(band, noise, previous, current, coupling)


def on_device(
    kernel_tiles, tile_rows, tile_cols, tile_counts, noise, prev_block, current_block, prev_coupling
):
    band = build_band(kernel_tiles[0, 0], tile_rows[0], tile_cols[0], tile_counts)
    following, diag_t, upper = lanczos(band, noise[None, :], prev_block, current_block, prev_coupling)
    return (following, jnp.swapaxes(diag_t, 1, 2), jnp.swapaxes(upper, 1, 2))


def solution(mesh):
    in_specs = (
        P("row", "col", None, None, None),
        P("row", "col", None),
        P("row", "col", None),
        P("row", "col"),
        P(("row", "col")),
        P(None, ("row", "col")),
        P(None, ("row", "col")),
        P(),
    )
    out_specs = (P(None, ("row", "col")), P(), P())
    return jax.shard_map(
        on_device, mesh=mesh, in_specs=in_specs, out_specs=out_specs, check_vma=False
    )
```

```python
import jax
import jax.numpy as jnp
from jax import lax
from jax.experimental import pallas as pl
from jax.experimental.pallas import tpu as pltpu
from jax.sharding import PartitionSpec as P

ITERS = 6
K = 32
BS = 128
WIDTH = 256
N_ROW = 16
N_COL = 16
SLOTS = 128
PLANE = 8
MESH_IDS = pl.DeviceIdType.MESH
F32 = jnp.float32
BF16 = jnp.bfloat16


def dot_nn(left, right):
    return lax.dot_general(
        left, right, (((1,), (0,)), ((), ())), precision=lax.Precision.HIGHEST, preferred_element_type=F32
    )


def dot_nt(left, right):
    return lax.dot_general(
        left, right, (((1,), (1,)), ((), ())), precision=lax.Precision.HIGHEST, preferred_element_type=F32
    )


def band_kernel(rows_ref, cols_ref, count_ref, tiles, band_ref, total):
    def clear(i, carry):
        total[i] = jnp.zeros(total.shape[1:], F32)
        return carry

    lax.fori_loop(0, 2 * N_COL, clear, 0)
    first_col = 2 * (lax.axis_index("row") - 1)
    count = count_ref[0, 0]

    def add(slot, carry):
        i = rows_ref[0, slot]
        j = cols_ref[0, slot] - first_col
        total[i, j] += tiles[slot].astype(F32)
        return carry

    lax.fori_loop(0, count, add, 0)

    def place(c, carry):
        for half in range(2):
            for j in range(6):
                band_ref[c, half * BS : (half + 1) * BS, j * BS : (j + 1) * BS] = total[
                    2 * c + half, j
                ].astype(BF16)
        return carry

    lax.fori_loop(0, N_COL, place, 0)


def build_band(tiles, rows, cols, count):
    smem = pl.BlockSpec(memory_space=pltpu.SMEM)
    return pl.pallas_call(
        band_kernel,
        out_shape=jax.ShapeDtypeStruct((N_COL, 2 * BS, 6 * BS), BF16),
        in_specs=[smem, smem, smem, pl.BlockSpec(memory_space=pltpu.VMEM)],
        out_specs=pl.BlockSpec(memory_space=pltpu.VMEM),
        scratch_shapes=[
            pltpu.VMEM((2 * N_COL, 6, BS, BS), F32),
        ],
        compiler_params=pltpu.CompilerParams(vmem_limit_bytes=40 * 2**20),
        name="band",
    )(rows, cols, count, tiles)


def factor(gram):
    groups = K // 8
    sub = lax.broadcasted_iota(jnp.int32, (8, K), 0)
    lane = lax.broadcasted_iota(jnp.int32, (8, K), 1)
    g = [gram[8 * b : 8 * b + 8] for b in range(groups)]
    e = [jnp.where(lane == sub + 8 * b, 1.0, 0.0).astype(F32) for b in range(groups)]
    step = 4
    for base in range(0, K, step):
        a = base // 8
        spread = [
            [
                jnp.broadcast_to(g[b][:, base + j : base + j + 1], (8, K)) if b >= a else None
                for b in range(groups)
            ]
            for j in range(step)
        ]
        for j in range(step):
            s = (base + j) % 8
            pivot = spread[j][a][s : s + 1]
            guess = lax.rsqrt(pivot)
            scale = guess * (1.5 - 0.5 * (pivot * guess) * guess)
            g_row = g[a][s : s + 1] * scale
            e_row = e[a][s : s + 1] * scale
            later = {jj: spread[jj][a][s : s + 1] * scale for jj in range(j + 1, step)}
            for b in range(a, groups):
                part = spread[j][b] * scale
                if b == a:
                    part = jnp.where(sub > s, part, 0.0)
                g[b] = g[b] - part * g_row
                e[b] = e[b] - part * e_row
                for jj in range(j + 1, step):
                    spread[jj][b] = spread[jj][b] - part * later[jj]
            g[a] = jnp.where(sub == s, g_row, g[a])
            e[a] = jnp.where(sub == s, e_row, e[a])
    upper = [jnp.where(lane >= sub + 8 * b, g[b], 0.0) for b in range(groups)]
    return jnp.concatenate(upper, axis=0), jnp.concatenate(e, axis=0)


def lanczos_kernel(
    band, noise_ref, prev_ref, cur_ref, coup_ref,
    out_ref, diag_ref, upper_ref,
    ty, known, held, split, xband, xrows, facc, fsend, fown, frecv, zsend, zrecv, msend, mrecv, mir,
    hloc, h1, s2, h2, h3,
    send_sems, recv_sems, sum_send, sum_recv,
):
    r = lax.axis_index("row")
    c = lax.axis_index("col")
    x, zl = r // 4, r % 4
    zh, p = c // PLANE, c % PLANE
    z = zh * 4 + zl
    m = x * 8 + z
    up = (lax.rem(r + 1, N_ROW), c)
    down = (lax.rem(r + N_ROW - 1, N_ROW), c)
    over = (r, lax.rem(c + PLANE, N_COL))

    def plane_dev(pp):
        return (r, zh * PLANE + pp)

    def sheet_dev(d):
        xx = lax.rem(x + 2 + d // 8, 4)
        zz = lax.rem(z + 4 + d % 8, 8)
        return (xx * 4 + zz % 4, (zz // 4) * PLANE + p)

    def on_plane(body):
        lax.fori_loop(1, PLANE, lambda d, carry: (body(d, lax.rem(p + d, PLANE)), carry)[1], 0)

    def on_sheet(body):
        lax.fori_loop(0, 20, lambda d, carry: (body(sheet_dev(d)), carry)[1], 0)
        lax.fori_loop(21, 32, lambda d, carry: (body(sheet_dev(d)), carry)[1], 0)

    def put(src, dst, send, recv, dev):
        pltpu.make_async_remote_copy(
            src_ref=src, dst_ref=dst, send_sem=send, recv_sem=recv, device_id=dev, device_id_type=MESH_IDS
        ).start()

    def take(ref, sem):
        pltpu.make_async_copy(ref, ref, sem).wait()

    barrier = pltpu.get_barrier_semaphore()

    def greet(dev):
        pl.semaphore_signal(barrier, inc=1, device_id=dev, device_id_type=MESH_IDS)

    on_sheet(greet)
    on_plane(lambda d, pp: greet(plane_dev(pp)))
    ty[...] = jnp.zeros_like(ty)
    ty[K : 2 * K, :WIDTH] = cur_ref[...]
    ty[2 * K :, :WIDTH] = prev_ref[...]
    known[0] = coup_ref[...]
    pl.semaphore_wait(barrier, 7 + 31)


    def spread(n, par):
        own = xband.at[par, 1, pl.ds(0, n)]
        put(own, xband.at[par, 0, pl.ds(0, n)], send_sems.at[0], recv_sems.at[par, 0], up)
        put(own, xband.at[par, 2, pl.ds(0, n)], send_sems.at[0], recv_sems.at[par, 0], down)
        place = xrows.at[par, zh, p, pl.ds(0, n)]
        put(own, place, send_sems.at[1], recv_sems.at[par, 1], over)
        on_plane(lambda d, pp: put(own, place, send_sems.at[2], recv_sems.at[par, 2], plane_dev(pp)))
        xrows[par, zh, p, :n] = xband[par, 1, :n]

    def own_forward(n, par):
        def body(k, carry):
            for u in range(4):
                facc[4 * k + u, :n] = lax.dot_general(
                    xband[par, 1, :n], band[4 * k + u, :, WIDTH : 2 * WIDTH], (((1,), (1,)), ((), ())),
                    preferred_element_type=F32,
                )
            return carry

        lax.fori_loop(0, 4, body, 0)

    def pass_on(n, par):
        take(xband.at[par, pl.ds(0, 2), pl.ds(0, n)], recv_sems.at[par, 0])
        take(zrecv.at[par, pl.ds(0, n)], recv_sems.at[par, 1])
        other = xrows.at[par, 1 - zh, p, pl.ds(0, n)]
        on_plane(lambda d, pp: put(other, other, send_sems.at[3], recv_sems.at[par, 3], plane_dev(pp)))

    def forward(n, par, half):
        hi = 1 - zh if half == 0 else zh

        def product(pp):
            acc = facc[hi * PLANE + pp, :n]
            for g in (0, 2):
                acc = acc + lax.dot_general(
                    xband[par, g, :n], band[hi * PLANE + pp, :, g * WIDTH : (g + 1) * WIDTH],
                    (((1,), (1,)), ((), ())), preferred_element_type=F32,
                )
            return acc

        def send(d):
            put(
                fsend.at[half, d - 1, pl.ds(0, n)], frecv.at[par, half, d - 1, pl.ds(0, n)],
                send_sems.at[4 + half], recv_sems.at[par, 4 + half], plane_dev(lax.rem(p + d, PLANE)),
            )

        for first in (1, 5):
            parts = [product(lax.rem(p + first + u, PLANE)) for u in range(4)]
            for u in range(4):
                if first + u < PLANE:
                    fsend[half, first + u - 1, :n] = parts[u].astype(BF16)
                    send(first + u)
                else:
                    fown[half, :n] = parts[u]

    def seven(n):
        return xrows.at[0, 0, pl.ds(0, 7), pl.ds(0, n)]

    def mirror(n, par, hi, first):
        def body(k, carry):
            acc = None
            for u in range(4):
                pp = 4 * k + u
                term = jnp.dot(
                    xrows[par, hi, pp, :n], band[hi * PLANE + pp], preferred_element_type=F32
                )
                acc = term if acc is None else acc + term
            if first:
                mir[:n] = jnp.where(k == 0, acc, mir[:n] + acc)
            else:
                mir[:n] += acc
            return carry

        lax.fori_loop(0, 2, body, 0)

    def mirror_near(n, par):
        take(seven(n), recv_sems.at[par, 2])
        mirror(n, par, zh, True)

    def mirror_far(n, par):
        take(seven(n), recv_sems.at[par, 3])
        mirror(n, par, 1 - zh, False)
        msend[0, :n] = mir[:n, :WIDTH].astype(BF16)
        msend[1, :n] = mir[:n, 2 * WIDTH :].astype(BF16)
        for g, dev in ((0, down), (1, up)):
            put(
                msend.at[g, pl.ds(0, n)], mrecv.at[par, g, pl.ds(0, n)],
                send_sems.at[6], recv_sems.at[par, 6], dev,
            )

    def total(n, par, half):
        take(frecv.at[par, half, :, pl.ds(0, n)], recv_sems.at[par, 4 + half])
        acc = fown[half, :n]
        for d in range(7):
            acc = acc + frecv[par, half, d, :n].astype(F32)
        return acc

    def send_over(n, par):
        zsend[:n] = total(n, par, 0).astype(BF16)
        put(
            zsend.at[pl.ds(0, n)], zrecv.at[par, pl.ds(0, n)], send_sems.at[7], recv_sems.at[par, 7], over
        )

    def image_here(n, par, vectors):
        return total(n, par, 1) + mir[:n, WIDTH : 2 * WIDTH] + noise_ref[...] * vectors

    def image_whole(n, par, acc):
        take(mrecv.at[par, :, pl.ds(0, n)], recv_sems.at[par, 6])
        acc = acc + mrecv[par, 0, :n].astype(F32) + mrecv[par, 1, :n].astype(F32)
        take(zrecv.at[par, pl.ds(0, n)], recv_sems.at[par, 7])
        return acc + zrecv[par, :n].astype(F32)

    def all_left(n):
        one = zsend.at[pl.ds(0, n)]
        take(msend.at[:, pl.ds(0, n)], send_sems.at[0])
        take(one, send_sems.at[1])
        take(seven(n), send_sems.at[2])
        take(seven(n), send_sems.at[3])
        take(seven(n), send_sems.at[4])
        take(seven(n), send_sems.at[5])
        take(msend.at[:, pl.ds(0, n)], send_sems.at[6])
        take(one, send_sems.at[7])


    def sum_first(part):
        for k in range(PLANE):
            hloc[k] = part[4 * k : 4 * k + 4]
        on_plane(lambda d, pp: put(hloc.at[pp], h1.at[p], sum_send.at[0], sum_recv.at[0], plane_dev(pp)))
        h1[p] = hloc[p]

    def sum_second(par):
        take(h1.at[pl.ds(0, 7)], sum_recv.at[0])
        piece = jnp.sum(h1[...], axis=0)
        s2[...] = piece
        h2[par, m] = piece
        on_sheet(lambda dev: put(s2, h2.at[par, m], sum_send.at[1], sum_recv.at[1 + par], dev))

    def sum_third(par):
        take(h2.at[par, pl.ds(0, 31)], sum_recv.at[1 + par])
        h3[p] = jnp.sum(h2[par], axis=0)
        on_plane(lambda d, pp: put(h3.at[p], h3.at[p], sum_send.at[2], sum_recv.at[3], plane_dev(pp)))

    def sum_result():
        take(h1.at[pl.ds(0, 7)], sum_recv.at[3])
        h = jnp.concatenate([h3[k] for k in range(PLANE)], axis=0)
        h = h * (1.0 / (N_ROW * N_COL * WIDTH))
        return [h[:, k * K : (k + 1) * K] for k in range(3)]

    def sum_left(par):
        take(h1.at[pl.ds(0, 7)], sum_send.at[0])
        take(h2.at[par, pl.ds(0, 31)], sum_send.at[1])
        take(h1.at[pl.ds(0, 7)], sum_send.at[2])

    lane = lax.broadcasted_iota(jnp.int32, (K, 4 * K), 1)

    def split_in_three(value, start):
        for k in range(3):
            part = value.astype(BF16)
            split[k, start : start + K] = part
            value = value - part.astype(F32)

    split[...] = jnp.zeros_like(split)
    split_in_three(cur_ref[...], 0)
    split_in_three(prev_ref[...], K)

    xband[1, 1, :K] = cur_ref[...].astype(BF16)
    xband[1, 1, K:] = prev_ref[...].astype(BF16)
    spread(2 * K, 1)
    q_and_p = ty[K:, :WIDTH]
    both = dot_nt(q_and_p, jnp.concatenate([q_and_p, ty[2 * K :, :WIDTH], ty[2 * K :, :WIDTH]], axis=0))
    sum_first(jnp.where(lane < 2 * K, both[:K], both[K:]))
    own_forward(2 * K, 1)
    sum_second(1)
    pass_on(2 * K, 1)
    forward(2 * K, 1, 0)
    forward(2 * K, 1, 1)
    mirror_near(2 * K, 1)
    mirror_far(2 * K, 1)
    send_over(2 * K, 1)
    sum_third(1)
    images = image_whole(2 * K, 1, image_here(2 * K, 1, ty[K:, :WIDTH]))
    ty[K:, WIDTH:] = images
    xband[0, 1, :K] = images[:K].astype(BF16)
    ty[:K, :WIDTH] = xband[0, 1, :K].astype(F32)
    all_left(2 * K)
    for k, value in enumerate(sum_result()):
        known[1 + k] = value
    sum_left(1)

    def iteration(it, carry):
        par = lax.rem(it, 2)
        more = it < ITERS - 1

        image = xband[par, 1, :K]
        split[0, 2 * K : 3 * K] = image
        terms = [
            lax.dot_general(
                image, split[k], (((1,), (1,)), ((), ())), preferred_element_type=F32
            )
            for k in range(3)
        ]
        sum_first(terms[0] + terms[1] + terms[2])

        @pl.when(more)
        def _():
            spread(K, par)

        @pl.when(it > 0)
        def _():
            known[3] = known[1]
            known[1] = dot_nt(dot_nn(held[0], held[1]), held[0])
            known[2] = dot_nn(held[0], held[2])

        b, q_q, q_p, p_p = (known[k] for k in range(4))
        b_qp = dot_nt(b, q_p)
        b_pp = b - dot_nn(b, p_p)
        q_rest = q_q - dot_nt(q_p, q_p)
        p_rest = q_p - dot_nn(q_p, p_p)

        @pl.when(more)
        def _():
            own_forward(K, par)

        sum_second(par)

        @pl.when(more)
        def _():
            pass_on(K, par)
            forward(K, par, 0)
            forward(K, par, 1)
            mirror_near(K, par)

        sum_third(par)

        @pl.when(more)
        def _():
            mirror_far(K, par)
            send_over(K, par)
            ty[:K, WIDTH:] = image_here(K, par, ty[:K, :WIDTH])

        im_q, im_p, im_im = sum_result()
        diag_t = im_q - b_qp
        back = im_p + b_pp
        cp = back - dot_nn(diag_t, q_p)
        t_q = im_q - dot_nt(back, q_p) - dot_nn(diag_t, q_rest)
        t_p = im_p - dot_nn(back, p_p) - dot_nn(diag_t, p_rest)
        gram = im_im - dot_nt(diag_t, im_q) - dot_nt(cp, im_p) - dot_nt(t_q, diag_t) - dot_nt(t_p, cp)
        rest = dot_nn(cp, ty[2 * K :]) + dot_nn(diag_t, ty[K : 2 * K])
        upper, inverse = factor(gram)

        @pl.when(more)
        def _():
            ty[:K, WIDTH:] = image_whole(K, par, ty[:K, WIDTH:])

        following = dot_nn(inverse, ty[:K] - rest)
        rounded = following[:, WIDTH:].astype(BF16)
        xband[1 - par, 1, :K] = rounded
        for k in range(3):
            split[k, K : 2 * K] = split[k, :K]
        split_in_three(following[:, :WIDTH], 0)
        ty[2 * K :] = ty[K : 2 * K]
        ty[K : 2 * K] = following
        ty[:K, :WIDTH] = rounded.astype(F32)
        diag_ref[it] = diag_t
        upper_ref[it] = upper
        known[0] = upper
        held[0] = inverse
        held[1] = gram
        held[2] = t_q

        @pl.when(more)
        def _():
            all_left(K)

        sum_left(par)
        return carry

    lax.fori_loop(0, ITERS, iteration, 0)
    out_ref[...] = ty[K : 2 * K, :WIDTH]


def lanczos(band, noise, previous, current, coupling):
    vmem = pl.BlockSpec(memory_space=pltpu.VMEM)
    panel = (K, WIDTH)
    two = (2 * K, WIDTH)
    piece = (4, 4 * K)
    return pl.pallas_call(
        lanczos_kernel,
        out_shape=(
            jax.ShapeDtypeStruct(panel, F32),
            jax.ShapeDtypeStruct((ITERS, K, K), F32),
            jax.ShapeDtypeStruct((ITERS, K, K), F32),
        ),
        in_specs=[vmem, vmem, vmem, vmem, vmem],
        out_specs=(vmem, vmem, vmem),
        scratch_shapes=[
            pltpu.VMEM((3 * K, 2 * WIDTH), F32),
            pltpu.VMEM((4, K, K), F32),
            pltpu.VMEM((3, K, K), F32),
            pltpu.VMEM((3, 4 * K, WIDTH), BF16),
            pltpu.VMEM((2, 3) + two, BF16),
            pltpu.VMEM((2, 2, PLANE) + two, BF16),
            pltpu.VMEM((N_COL,) + two, F32),
            pltpu.VMEM((2, 7) + two, BF16),
            pltpu.VMEM((2,) + two, F32),
            pltpu.VMEM((2, 2, 7) + two, BF16),
            pltpu.VMEM(two, BF16),
            pltpu.VMEM((2,) + two, BF16),
            pltpu.VMEM((2,) + two, BF16),
            pltpu.VMEM((2, 2) + two, BF16),
            pltpu.VMEM((2 * K, 3 * WIDTH), F32),
            pltpu.VMEM((8,) + piece, F32),
            pltpu.VMEM((8,) + piece, F32),
            pltpu.VMEM(piece, F32),
            pltpu.VMEM((2, 32) + piece, F32),
            pltpu.VMEM((8,) + piece, F32),
            pltpu.SemaphoreType.DMA((8,)),
            pltpu.SemaphoreType.DMA((2, 8)),
            pltpu.SemaphoreType.DMA((3,)),
            pltpu.SemaphoreType.DMA((4,)),
        ],
        compiler_params=pltpu.CompilerParams(
            collective_id=0, has_side_effects=True, vmem_limit_bytes=40 * 2**20
        ),
        name="lanczos",
    )(band, noise, previous, current, coupling)


def on_device(
    kernel_tiles, tile_rows, tile_cols, tile_counts, noise, prev_block, current_block, prev_coupling
):
    band = build_band(kernel_tiles[0, 0], tile_rows[0], tile_cols[0], tile_counts)
    following, diag_t, upper = lanczos(band, noise[None, :], prev_block, current_block, prev_coupling)
    return (following, jnp.swapaxes(diag_t, 1, 2), jnp.swapaxes(upper, 1, 2))


def solution(mesh):
    in_specs = (
        P("row", "col", None, None, None),
        P("row", "col", None),
        P("row", "col", None),
        P("row", "col"),
        P(("row", "col")),
        P(None, ("row", "col")),
        P(None, ("row", "col")),
        P(),
    )
    out_specs = (P(None, ("row", "col")), P(), P())
    return jax.shard_map(
        on_device, mesh=mesh, in_specs=in_specs, out_specs=out_specs, check_vma=False
    )
```

```python
import jax
import jax.numpy as jnp
from jax import lax
from jax.experimental import pallas as pl
from jax.experimental.pallas import tpu as pltpu
from jax.sharding import PartitionSpec as P

ITERS = 6
K = 32
BS = 128
WIDTH = 256
N_ROW = 16
N_COL = 16
SLOTS = 128
PLANE = 8
MESH_IDS = pl.DeviceIdType.MESH
F32 = jnp.float32
BF16 = jnp.bfloat16


def dot_nn(left, right):
    return lax.dot_general(
        left, right, (((1,), (0,)), ((), ())), precision=lax.Precision.HIGHEST, preferred_element_type=F32
    )


def dot_nt(left, right):
    return lax.dot_general(
        left, right, (((1,), (1,)), ((), ())), precision=lax.Precision.HIGHEST, preferred_element_type=F32
    )


def band_kernel(rows_ref, cols_ref, count_ref, tiles, band_ref, total):
    def clear(i, carry):
        total[i] = jnp.zeros(total.shape[1:], F32)
        return carry

    lax.fori_loop(0, 2 * N_COL, clear, 0)
    first_col = 2 * (lax.axis_index("row") - 1)
    count = count_ref[0, 0]

    def add(slot, carry):
        i = rows_ref[0, slot]
        j = cols_ref[0, slot] - first_col
        total[i, j] += tiles[slot].astype(F32)
        return carry

    lax.fori_loop(0, count, add, 0)

    def place(c, carry):
        for half in range(2):
            for j in range(6):
                band_ref[c, half * BS : (half + 1) * BS, j * BS : (j + 1) * BS] = total[
                    2 * c + half, j
                ].astype(BF16)
        return carry

    lax.fori_loop(0, N_COL, place, 0)


def build_band(tiles, rows, cols, count):
    smem = pl.BlockSpec(memory_space=pltpu.SMEM)
    return pl.pallas_call(
        band_kernel,
        out_shape=jax.ShapeDtypeStruct((N_COL, 2 * BS, 6 * BS), BF16),
        in_specs=[smem, smem, smem, pl.BlockSpec(memory_space=pltpu.VMEM)],
        out_specs=pl.BlockSpec(memory_space=pltpu.VMEM),
        scratch_shapes=[
            pltpu.VMEM((2 * N_COL, 6, BS, BS), F32),
        ],
        compiler_params=pltpu.CompilerParams(vmem_limit_bytes=40 * 2**20),
        name="band",
    )(rows, cols, count, tiles)


def factor(gram):
    groups = K // 8
    sub = lax.broadcasted_iota(jnp.int32, (8, K), 0)
    lane = lax.broadcasted_iota(jnp.int32, (8, K), 1)
    g = [gram[8 * b : 8 * b + 8] for b in range(groups)]
    e = [jnp.where(lane == sub + 8 * b, 1.0, 0.0).astype(F32) for b in range(groups)]
    step = 4
    for base in range(0, K, step):
        a = base // 8
        spread = [
            [
                jnp.broadcast_to(g[b][:, base + j : base + j + 1], (8, K)) if b >= a else None
                for b in range(groups)
            ]
            for j in range(step)
        ]
        for j in range(step):
            s = (base + j) % 8
            pivot = spread[j][a][s : s + 1]
            guess = lax.rsqrt(pivot)
            scale = guess * (1.5 - 0.5 * (pivot * guess) * guess)
            g_row = g[a][s : s + 1] * scale
            e_row = e[a][s : s + 1] * scale
            later = {jj: spread[jj][a][s : s + 1] * scale for jj in range(j + 1, step)}
            for b in range(a, groups):
                part = spread[j][b] * scale
                if b == a:
                    part = jnp.where(sub > s, part, 0.0)
                g[b] = g[b] - part * g_row
                e[b] = e[b] - part * e_row
                for jj in range(j + 1, step):
                    spread[jj][b] = spread[jj][b] - part * later[jj]
            g[a] = jnp.where(sub == s, g_row, g[a])
            e[a] = jnp.where(sub == s, e_row, e[a])
    upper = [jnp.where(lane >= sub + 8 * b, g[b], 0.0) for b in range(groups)]
    return jnp.concatenate(upper, axis=0), jnp.concatenate(e, axis=0)


def lanczos_kernel(
    band, noise_ref, prev_ref, cur_ref, coup_ref,
    out_ref, diag_ref, upper_ref,
    ty, known, held, split, xband, xrows, facc, fsend, fown, frecv, zsend, zrecv, msend, mrecv, mir,
    hloc, h1, s2, h2, h3,
    send_sems, recv_sems, sum_send, sum_recv,
):
    r = lax.axis_index("row")
    c = lax.axis_index("col")
    x, zl = r // 4, r % 4
    zh, p = c // PLANE, c % PLANE
    z = zh * 4 + zl
    m = x * 8 + z
    up = (lax.rem(r + 1, N_ROW), c)
    down = (lax.rem(r + N_ROW - 1, N_ROW), c)
    over = (r, lax.rem(c + PLANE, N_COL))

    def plane_dev(pp):
        return (r, zh * PLANE + pp)

    def sheet_dev(d):
        xx = lax.rem(x + 2 + d // 8, 4)
        zz = lax.rem(z + 4 + d % 8, 8)
        return (xx * 4 + zz % 4, (zz // 4) * PLANE + p)

    def on_plane(body):
        lax.fori_loop(3, PLANE, lambda d, carry: (body(d, lax.rem(p + d, PLANE)), carry)[1], 0)
        lax.fori_loop(1, 3, lambda d, carry: (body(d, lax.rem(p + d, PLANE)), carry)[1], 0)

    def on_sheet(body):
        lax.fori_loop(0, 20, lambda d, carry: (body(sheet_dev(d)), carry)[1], 0)
        lax.fori_loop(21, 32, lambda d, carry: (body(sheet_dev(d)), carry)[1], 0)

    def put(src, dst, send, recv, dev):
        pltpu.make_async_remote_copy(
            src_ref=src, dst_ref=dst, send_sem=send, recv_sem=recv, device_id=dev, device_id_type=MESH_IDS
        ).start()

    def take(ref, sem):
        pltpu.make_async_copy(ref, ref, sem).wait()

    barrier = pltpu.get_barrier_semaphore()

    def greet(dev):
        pl.semaphore_signal(barrier, inc=1, device_id=dev, device_id_type=MESH_IDS)

    on_sheet(greet)
    on_plane(lambda d, pp: greet(plane_dev(pp)))
    ty[...] = jnp.zeros_like(ty)
    ty[K : 2 * K, :WIDTH] = cur_ref[...]
    ty[2 * K :, :WIDTH] = prev_ref[...]
    known[0] = coup_ref[...]
    pl.semaphore_wait(barrier, 7 + 31)


    def spread(n, par):
        own = xband.at[par, 1, pl.ds(0, n)]
        put(own, xband.at[par, 0, pl.ds(0, n)], send_sems.at[0], recv_sems.at[par, 0], up)
        put(own, xband.at[par, 2, pl.ds(0, n)], send_sems.at[0], recv_sems.at[par, 0], down)
        place = xrows.at[par, zh, p, pl.ds(0, n)]
        put(own, place, send_sems.at[1], recv_sems.at[par, 1], over)
        on_plane(lambda d, pp: put(own, place, send_sems.at[2], recv_sems.at[par, 2], plane_dev(pp)))
        xrows[par, zh, p, :n] = xband[par, 1, :n]

    def own_forward(n, par):
        def body(k, carry):
            for u in range(4):
                facc[4 * k + u, :n] = lax.dot_general(
                    xband[par, 1, :n], band[4 * k + u, :, WIDTH : 2 * WIDTH], (((1,), (1,)), ((), ())),
                    preferred_element_type=F32,
                )
            return carry

        lax.fori_loop(0, 4, body, 0)

    def pass_on(n, par):
        take(xband.at[par, pl.ds(0, 2), pl.ds(0, n)], recv_sems.at[par, 0])
        take(zrecv.at[par, pl.ds(0, n)], recv_sems.at[par, 1])
        other = xrows.at[par, 1 - zh, p, pl.ds(0, n)]
        on_plane(lambda d, pp: put(other, other, send_sems.at[3], recv_sems.at[par, 3], plane_dev(pp)))

    def forward(n, par, half):
        hi = 1 - zh if half == 0 else zh

        def product(pp):
            acc = facc[hi * PLANE + pp, :n]
            for g in (0, 2):
                acc = acc + lax.dot_general(
                    xband[par, g, :n], band[hi * PLANE + pp, :, g * WIDTH : (g + 1) * WIDTH],
                    (((1,), (1,)), ((), ())), preferred_element_type=F32,
                )
            return acc

        def send(d):
            put(
                fsend.at[half, d - 1, pl.ds(0, n)], frecv.at[par, half, d - 1, pl.ds(0, n)],
                send_sems.at[4 + half], recv_sems.at[par, 4 + half], plane_dev(lax.rem(p + d, PLANE)),
            )

        for first in (1, 5):
            parts = [product(lax.rem(p + first + u, PLANE)) for u in range(4)]
            for u in range(4):
                if first + u < PLANE:
                    fsend[half, first + u - 1, :n] = parts[u].astype(BF16)
                    send(first + u)
                else:
                    fown[half, :n] = parts[u]

    def seven(n):
        return xrows.at[0, 0, pl.ds(0, 7), pl.ds(0, n)]

    def mirror(n, par, hi, first):
        def body(k, carry):
            acc = None
            for u in range(4):
                pp = 4 * k + u
                term = jnp.dot(
                    xrows[par, hi, pp, :n], band[hi * PLANE + pp], preferred_element_type=F32
                )
                acc = term if acc is None else acc + term
            if first:
                mir[:n] = jnp.where(k == 0, acc, mir[:n] + acc)
            else:
                mir[:n] += acc
            return carry

        lax.fori_loop(0, 2, body, 0)

    def mirror_near(n, par):
        take(seven(n), recv_sems.at[par, 2])
        mirror(n, par, zh, True)

    def mirror_far(n, par):
        take(seven(n), recv_sems.at[par, 3])
        mirror(n, par, 1 - zh, False)
        msend[0, :n] = mir[:n, :WIDTH].astype(BF16)
        msend[1, :n] = mir[:n, 2 * WIDTH :].astype(BF16)
        for g, dev in ((0, down), (1, up)):
            put(
                msend.at[g, pl.ds(0, n)], mrecv.at[par, g, pl.ds(0, n)],
                send_sems.at[6], recv_sems.at[par, 6], dev,
            )

    def total(n, par, half):
        take(frecv.at[par, half, :, pl.ds(0, n)], recv_sems.at[par, 4 + half])
        acc = fown[half, :n]
        for d in range(7):
            acc = acc + frecv[par, half, d, :n].astype(F32)
        return acc

    def send_over(n, par):
        zsend[:n] = total(n, par, 0).astype(BF16)
        put(
            zsend.at[pl.ds(0, n)], zrecv.at[par, pl.ds(0, n)], send_sems.at[7], recv_sems.at[par, 7], over
        )

    def image_here(n, par, vectors):
        return total(n, par, 1) + mir[:n, WIDTH : 2 * WIDTH] + noise_ref[...] * vectors

    def image_whole(n, par, acc):
        take(mrecv.at[par, :, pl.ds(0, n)], recv_sems.at[par, 6])
        acc = acc + mrecv[par, 0, :n].astype(F32) + mrecv[par, 1, :n].astype(F32)
        take(zrecv.at[par, pl.ds(0, n)], recv_sems.at[par, 7])
        return acc + zrecv[par, :n].astype(F32)

    def all_left(n):
        one = zsend.at[pl.ds(0, n)]
        take(msend.at[:, pl.ds(0, n)], send_sems.at[0])
        take(one, send_sems.at[1])
        take(seven(n), send_sems.at[2])
        take(seven(n), send_sems.at[3])
        take(seven(n), send_sems.at[4])
        take(seven(n), send_sems.at[5])
        take(msend.at[:, pl.ds(0, n)], send_sems.at[6])
        take(one, send_sems.at[7])


    def sum_first(part):
        for k in range(PLANE):
            hloc[k] = part[4 * k : 4 * k + 4]
        on_plane(lambda d, pp: put(hloc.at[pp], h1.at[p], sum_send.at[0], sum_recv.at[0], plane_dev(pp)))
        h1[p] = hloc[p]

    def sum_second(par):
        take(h1.at[pl.ds(0, 7)], sum_recv.at[0])
        piece = jnp.sum(h1[...], axis=0)
        s2[...] = piece
        h2[par, m] = piece
        on_sheet(lambda dev: put(s2, h2.at[par, m], sum_send.at[1], sum_recv.at[1 + par], dev))

    def sum_third(par):
        take(h2.at[par, pl.ds(0, 31)], sum_recv.at[1 + par])
        h3[p] = jnp.sum(h2[par], axis=0)
        on_plane(lambda d, pp: put(h3.at[p], h3.at[p], sum_send.at[2], sum_recv.at[3], plane_dev(pp)))

    def sum_result():
        take(h1.at[pl.ds(0, 7)], sum_recv.at[3])
        h = jnp.concatenate([h3[k] for k in range(PLANE)], axis=0)
        h = h * (1.0 / (N_ROW * N_COL * WIDTH))
        return [h[:, k * K : (k + 1) * K] for k in range(3)]

    def sum_left(par):
        take(h1.at[pl.ds(0, 7)], sum_send.at[0])
        take(h2.at[par, pl.ds(0, 31)], sum_send.at[1])

    lane = lax.broadcasted_iota(jnp.int32, (K, 4 * K), 1)

    def split_in_three(value, start):
        for k in range(3):
            part = value.astype(BF16)
            split[k, start : start + K] = part
            value = value - part.astype(F32)

    split[...] = jnp.zeros_like(split)
    split_in_three(cur_ref[...], 0)
    split_in_three(prev_ref[...], K)

    xband[1, 1, :K] = cur_ref[...].astype(BF16)
    xband[1, 1, K:] = prev_ref[...].astype(BF16)
    spread(2 * K, 1)
    q_and_p = ty[K:, :WIDTH]
    both = dot_nt(q_and_p, jnp.concatenate([q_and_p, ty[2 * K :, :WIDTH], ty[2 * K :, :WIDTH]], axis=0))
    sum_first(jnp.where(lane < 2 * K, both[:K], both[K:]))
    own_forward(2 * K, 1)
    sum_second(1)
    pass_on(2 * K, 1)
    forward(2 * K, 1, 0)
    forward(2 * K, 1, 1)
    mirror_near(2 * K, 1)
    mirror_far(2 * K, 1)
    send_over(2 * K, 1)
    sum_third(1)
    images = image_whole(2 * K, 1, image_here(2 * K, 1, ty[K:, :WIDTH]))
    ty[K:, WIDTH:] = images
    xband[0, 1, :K] = images[:K].astype(BF16)
    ty[:K, :WIDTH] = xband[0, 1, :K].astype(F32)
    all_left(2 * K)
    for k, value in enumerate(sum_result()):
        known[1 + k] = value
    sum_left(1)
    take(h1.at[pl.ds(0, 7)], sum_send.at[2])

    def iteration(it, carry):
        par = lax.rem(it, 2)
        more = it < ITERS - 1

        image = xband[par, 1, :K]
        split[0, 2 * K : 3 * K] = image
        terms = [
            lax.dot_general(
                image, split[k], (((1,), (1,)), ((), ())), preferred_element_type=F32
            )
            for k in range(3)
        ]
        sum_first(terms[0] + terms[1] + terms[2])

        @pl.when(more)
        def _():
            spread(K, par)

        @pl.when(it > 0)
        def _():
            known[3] = known[1]
            known[1] = dot_nt(dot_nn(held[0], held[1]), held[0])
            known[2] = dot_nn(held[0], held[2])

        b, q_q, q_p, p_p = (known[k] for k in range(4))
        b_qp = dot_nt(b, q_p)
        b_pp = b - dot_nn(b, p_p)
        q_rest = q_q - dot_nt(q_p, q_p)
        p_rest = q_p - dot_nn(q_p, p_p)

        @pl.when(more)
        def _():
            own_forward(K, par)

        sum_second(par)

        @pl.when(more)
        def _():
            pass_on(K, par)
            forward(K, par, 0)
            forward(K, par, 1)
            mirror_near(K, par)

        sum_third(par)

        @pl.when(more)
        def _():
            mirror_far(K, par)
            send_over(K, par)
            ty[:K, WIDTH:] = image_here(K, par, ty[:K, :WIDTH])
            all_left(K)

        sum_left(par)
        im_q, im_p, im_im = sum_result()
        diag_t = im_q - b_qp
        back = im_p + b_pp
        cp = back - dot_nn(diag_t, q_p)
        t_q = im_q - dot_nt(back, q_p) - dot_nn(diag_t, q_rest)
        t_p = im_p - dot_nn(back, p_p) - dot_nn(diag_t, p_rest)
        gram = im_im - dot_nt(diag_t, im_q) - dot_nt(cp, im_p) - dot_nt(t_q, diag_t) - dot_nt(t_p, cp)
        rest = dot_nn(cp, ty[2 * K :]) + dot_nn(diag_t, ty[K : 2 * K])
        upper, inverse = factor(gram)

        @pl.when(more)
        def _():
            ty[:K, WIDTH:] = image_whole(K, par, ty[:K, WIDTH:])

        following = dot_nn(inverse, ty[:K] - rest)
        rounded = following[:, WIDTH:].astype(BF16)
        xband[1 - par, 1, :K] = rounded
        for k in range(3):
            split[k, K : 2 * K] = split[k, :K]
        split_in_three(following[:, :WIDTH], 0)
        ty[2 * K :] = ty[K : 2 * K]
        ty[K : 2 * K] = following
        ty[:K, :WIDTH] = rounded.astype(F32)
        diag_ref[it] = diag_t
        upper_ref[it] = upper
        known[0] = upper
        held[0] = inverse
        held[1] = gram
        held[2] = t_q
        take(h1.at[pl.ds(0, 7)], sum_send.at[2])
        return carry

    lax.fori_loop(0, ITERS, iteration, 0)
    out_ref[...] = ty[K : 2 * K, :WIDTH]


def lanczos(band, noise, previous, current, coupling):
    vmem = pl.BlockSpec(memory_space=pltpu.VMEM)
    panel = (K, WIDTH)
    two = (2 * K, WIDTH)
    piece = (4, 4 * K)
    return pl.pallas_call(
        lanczos_kernel,
        out_shape=(
            jax.ShapeDtypeStruct(panel, F32),
            jax.ShapeDtypeStruct((ITERS, K, K), F32),
            jax.ShapeDtypeStruct((ITERS, K, K), F32),
        ),
        in_specs=[vmem, vmem, vmem, vmem, vmem],
        out_specs=(vmem, vmem, vmem),
        scratch_shapes=[
            pltpu.VMEM((3 * K, 2 * WIDTH), F32),
            pltpu.VMEM((4, K, K), F32),
            pltpu.VMEM((3, K, K), F32),
            pltpu.VMEM((3, 4 * K, WIDTH), BF16),
            pltpu.VMEM((2, 3) + two, BF16),
            pltpu.VMEM((2, 2, PLANE) + two, BF16),
            pltpu.VMEM((N_COL,) + two, F32),
            pltpu.VMEM((2, 7) + two, BF16),
            pltpu.VMEM((2,) + two, F32),
            pltpu.VMEM((2, 2, 7) + two, BF16),
            pltpu.VMEM(two, BF16),
            pltpu.VMEM((2,) + two, BF16),
            pltpu.VMEM((2,) + two, BF16),
            pltpu.VMEM((2, 2) + two, BF16),
            pltpu.VMEM((2 * K, 3 * WIDTH), F32),
            pltpu.VMEM((8,) + piece, F32),
            pltpu.VMEM((8,) + piece, F32),
            pltpu.VMEM(piece, F32),
            pltpu.VMEM((2, 32) + piece, F32),
            pltpu.VMEM((8,) + piece, F32),
            pltpu.SemaphoreType.DMA((8,)),
            pltpu.SemaphoreType.DMA((2, 8)),
            pltpu.SemaphoreType.DMA((3,)),
            pltpu.SemaphoreType.DMA((4,)),
        ],
        compiler_params=pltpu.CompilerParams(
            collective_id=0, has_side_effects=True, vmem_limit_bytes=40 * 2**20
        ),
        name="lanczos",
    )(band, noise, previous, current, coupling)


def on_device(
    kernel_tiles, tile_rows, tile_cols, tile_counts, noise, prev_block, current_block, prev_coupling
):
    band = build_band(kernel_tiles[0, 0], tile_rows[0], tile_cols[0], tile_counts)
    following, diag_t, upper = lanczos(band, noise[None, :], prev_block, current_block, prev_coupling)
    return (following, jnp.swapaxes(diag_t, 1, 2), jnp.swapaxes(upper, 1, 2))


def solution(mesh):
    in_specs = (
        P("row", "col", None, None, None),
        P("row", "col", None),
        P("row", "col", None),
        P("row", "col"),
        P(("row", "col")),
        P(None, ("row", "col")),
        P(None, ("row", "col")),
        P(),
    )
    out_specs = (P(None, ("row", "col")), P(), P())
    return jax.shard_map(
        on_device, mesh=mesh, in_specs=in_specs, out_specs=out_specs, check_vma=False
    )
```

```python
import jax
import jax.numpy as jnp
from jax import lax
from jax.experimental import pallas as pl
from jax.experimental.pallas import tpu as pltpu
from jax.sharding import PartitionSpec as P

ITERS = 6
K = 32
BS = 128
WIDTH = 256
N_ROW = 16
N_COL = 16
SLOTS = 128
PLANE = 8
MESH_IDS = pl.DeviceIdType.MESH
F32 = jnp.float32
BF16 = jnp.bfloat16


def dot_nn(left, right):
    return lax.dot_general(
        left, right, (((1,), (0,)), ((), ())), precision=lax.Precision.HIGHEST, preferred_element_type=F32
    )


def dot_nt(left, right):
    return lax.dot_general(
        left, right, (((1,), (1,)), ((), ())), precision=lax.Precision.HIGHEST, preferred_element_type=F32
    )


def band_kernel(rows_ref, cols_ref, count_ref, tiles, band_ref, total):
    def clear(i, carry):
        total[i] = jnp.zeros(total.shape[1:], F32)
        return carry

    lax.fori_loop(0, 2 * N_COL, clear, 0)
    first_col = 2 * (lax.axis_index("row") - 1)
    count = count_ref[0, 0]

    def add(slot, carry):
        i = rows_ref[0, slot]
        j = cols_ref[0, slot] - first_col
        total[i, j] += tiles[slot].astype(F32)
        return carry

    lax.fori_loop(0, count, add, 0)

    def place(c, carry):
        for half in range(2):
            for j in range(6):
                band_ref[c, half * BS : (half + 1) * BS, j * BS : (j + 1) * BS] = total[
                    2 * c + half, j
                ].astype(BF16)
        return carry

    lax.fori_loop(0, N_COL, place, 0)


def build_band(tiles, rows, cols, count):
    smem = pl.BlockSpec(memory_space=pltpu.SMEM)
    return pl.pallas_call(
        band_kernel,
        out_shape=jax.ShapeDtypeStruct((N_COL, 2 * BS, 6 * BS), BF16),
        in_specs=[smem, smem, smem, pl.BlockSpec(memory_space=pltpu.VMEM)],
        out_specs=pl.BlockSpec(memory_space=pltpu.VMEM),
        scratch_shapes=[
            pltpu.VMEM((2 * N_COL, 6, BS, BS), F32),
        ],
        compiler_params=pltpu.CompilerParams(vmem_limit_bytes=40 * 2**20),
        name="band",
    )(rows, cols, count, tiles)


def factor(gram):
    groups = K // 8
    sub = lax.broadcasted_iota(jnp.int32, (8, K), 0)
    lane = lax.broadcasted_iota(jnp.int32, (8, K), 1)
    g = [gram[8 * b : 8 * b + 8] for b in range(groups)]
    e = [jnp.where(lane == sub + 8 * b, 1.0, 0.0).astype(F32) for b in range(groups)]
    step = 4
    for base in range(0, K, step):
        a = base // 8
        spread = [
            [
                jnp.broadcast_to(g[b][:, base + j : base + j + 1], (8, K)) if b >= a else None
                for b in range(groups)
            ]
            for j in range(step)
        ]
        for j in range(step):
            s = (base + j) % 8
            pivot = spread[j][a][s : s + 1]
            guess = lax.rsqrt(pivot)
            scale = guess * (1.5 - 0.5 * (pivot * guess) * guess)
            g_row = g[a][s : s + 1] * scale
            e_row = e[a][s : s + 1] * scale
            later = {jj: spread[jj][a][s : s + 1] * scale for jj in range(j + 1, step)}
            for b in range(a, groups):
                part = spread[j][b] * scale
                if b == a:
                    part = jnp.where(sub > s, part, 0.0)
                g[b] = g[b] - part * g_row
                e[b] = e[b] - part * e_row
                for jj in range(j + 1, step):
                    spread[jj][b] = spread[jj][b] - part * later[jj]
            g[a] = jnp.where(sub == s, g_row, g[a])
            e[a] = jnp.where(sub == s, e_row, e[a])
    upper = [jnp.where(lane >= sub + 8 * b, g[b], 0.0) for b in range(groups)]
    return jnp.concatenate(upper, axis=0), jnp.concatenate(e, axis=0)


def lanczos_kernel(
    band, noise_ref, prev_ref, cur_ref, coup_ref,
    out_ref, diag_ref, upper_ref,
    ty, known, held, split, xband, xrows, facc, fsend, fown, frecv, zsend, zrecv, msend, mrecv, mir,
    hloc, h1, s2, h2, h3,
    send_sems, recv_sems, sum_send, sum_recv,
):
    r = lax.axis_index("row")
    c = lax.axis_index("col")
    x, zl = r // 4, r % 4
    zh, p = c // PLANE, c % PLANE
    z = zh * 4 + zl
    m = x * 8 + z
    up = (lax.rem(r + 1, N_ROW), c)
    down = (lax.rem(r + N_ROW - 1, N_ROW), c)
    over = (r, lax.rem(c + PLANE, N_COL))

    def plane_dev(pp):
        return (r, zh * PLANE + pp)

    def sheet_dev(d):
        xx = lax.rem(x + 2 + d // 8, 4)
        zz = lax.rem(z + 4 + d % 8, 8)
        return (xx * 4 + zz % 4, (zz // 4) * PLANE + p)

    def on_plane(body):
        lax.fori_loop(3, PLANE, lambda d, carry: (body(d, lax.rem(p + d, PLANE)), carry)[1], 0)
        lax.fori_loop(1, 3, lambda d, carry: (body(d, lax.rem(p + d, PLANE)), carry)[1], 0)

    def on_sheet(body):
        lax.fori_loop(0, 20, lambda d, carry: (body(sheet_dev(d)), carry)[1], 0)
        lax.fori_loop(21, 32, lambda d, carry: (body(sheet_dev(d)), carry)[1], 0)

    def put(src, dst, send, recv, dev):
        pltpu.make_async_remote_copy(
            src_ref=src, dst_ref=dst, send_sem=send, recv_sem=recv, device_id=dev, device_id_type=MESH_IDS
        ).start()

    def take(ref, sem):
        pltpu.make_async_copy(ref, ref, sem).wait()

    barrier = pltpu.get_barrier_semaphore()

    def greet(dev):
        pl.semaphore_signal(barrier, inc=1, device_id=dev, device_id_type=MESH_IDS)

    on_sheet(greet)
    on_plane(lambda d, pp: greet(plane_dev(pp)))
    ty[...] = jnp.zeros_like(ty)
    ty[K : 2 * K, :WIDTH] = cur_ref[...]
    ty[2 * K :, :WIDTH] = prev_ref[...]
    known[0] = coup_ref[...]


    def spread(n, par):
        own = xband.at[par, 1, pl.ds(0, n)]
        put(own, xband.at[par, 0, pl.ds(0, n)], send_sems.at[0], recv_sems.at[par, 0], up)
        put(own, xband.at[par, 2, pl.ds(0, n)], send_sems.at[0], recv_sems.at[par, 0], down)
        place = xrows.at[par, zh, p, pl.ds(0, n)]
        put(own, place, send_sems.at[1], recv_sems.at[par, 1], over)
        on_plane(lambda d, pp: put(own, place, send_sems.at[2], recv_sems.at[par, 2], plane_dev(pp)))
        xrows[par, zh, p, :n] = xband[par, 1, :n]

    def own_forward(n, par):
        def body(k, carry):
            for u in range(4):
                facc[4 * k + u, :n] = lax.dot_general(
                    xband[par, 1, :n], band[4 * k + u, :, WIDTH : 2 * WIDTH], (((1,), (1,)), ((), ())),
                    preferred_element_type=F32,
                )
            return carry

        lax.fori_loop(0, 4, body, 0)

    def pass_on(n, par):
        take(xband.at[par, pl.ds(0, 2), pl.ds(0, n)], recv_sems.at[par, 0])
        take(zrecv.at[par, pl.ds(0, n)], recv_sems.at[par, 1])
        other = xrows.at[par, 1 - zh, p, pl.ds(0, n)]
        on_plane(lambda d, pp: put(other, other, send_sems.at[3], recv_sems.at[par, 3], plane_dev(pp)))

    def forward(n, par, half):
        hi = 1 - zh if half == 0 else zh

        def product(pp):
            acc = facc[hi * PLANE + pp, :n]
            for g in (0, 2):
                acc = acc + lax.dot_general(
                    xband[par, g, :n], band[hi * PLANE + pp, :, g * WIDTH : (g + 1) * WIDTH],
                    (((1,), (1,)), ((), ())), preferred_element_type=F32,
                )
            return acc

        def send(d):
            put(
                fsend.at[half, d - 1, pl.ds(0, n)], frecv.at[par, half, d - 1, pl.ds(0, n)],
                send_sems.at[4 + half], recv_sems.at[par, 4 + half], plane_dev(lax.rem(p + d, PLANE)),
            )

        for first in (1, 5):
            parts = [product(lax.rem(p + first + u, PLANE)) for u in range(4)]
            for u in range(4):
                if first + u < PLANE:
                    fsend[half, first + u - 1, :n] = parts[u].astype(BF16)
                    send(first + u)
                else:
                    fown[half, :n] = parts[u]

    def seven(n):
        return xrows.at[0, 0, pl.ds(0, 7), pl.ds(0, n)]

    def mirror(n, par, hi, first):
        def body(k, carry):
            acc = None
            for u in range(4):
                pp = 4 * k + u
                term = jnp.dot(
                    xrows[par, hi, pp, :n], band[hi * PLANE + pp], preferred_element_type=F32
                )
                acc = term if acc is None else acc + term
            if first:
                mir[:n] = jnp.where(k == 0, acc, mir[:n] + acc)
            else:
                mir[:n] += acc
            return carry

        lax.fori_loop(0, 2, body, 0)

    def mirror_near(n, par):
        take(seven(n), recv_sems.at[par, 2])
        mirror(n, par, zh, True)

    def mirror_far(n, par):
        take(seven(n), recv_sems.at[par, 3])
        mirror(n, par, 1 - zh, False)
        msend[0, :n] = mir[:n, :WIDTH].astype(BF16)
        msend[1, :n] = mir[:n, 2 * WIDTH :].astype(BF16)
        for g, dev in ((0, down), (1, up)):
            put(
                msend.at[g, pl.ds(0, n)], mrecv.at[par, g, pl.ds(0, n)],
                send_sems.at[6], recv_sems.at[par, 6], dev,
            )

    def total(n, par, half):
        take(frecv.at[par, half, :, pl.ds(0, n)], recv_sems.at[par, 4 + half])
        acc = fown[half, :n]
        for d in range(7):
            acc = acc + frecv[par, half, d, :n].astype(F32)
        return acc

    def send_over(n, par):
        zsend[:n] = total(n, par, 0).astype(BF16)
        put(
            zsend.at[pl.ds(0, n)], zrecv.at[par, pl.ds(0, n)], send_sems.at[7], recv_sems.at[par, 7], over
        )

    def image_here(n, par, vectors):
        return total(n, par, 1) + mir[:n, WIDTH : 2 * WIDTH] + noise_ref[...] * vectors

    def image_whole(n, par, acc):
        take(mrecv.at[par, :, pl.ds(0, n)], recv_sems.at[par, 6])
        acc = acc + mrecv[par, 0, :n].astype(F32) + mrecv[par, 1, :n].astype(F32)
        take(zrecv.at[par, pl.ds(0, n)], recv_sems.at[par, 7])
        return acc + zrecv[par, :n].astype(F32)

    def all_left(n):
        one = zsend.at[pl.ds(0, n)]
        take(msend.at[:, pl.ds(0, n)], send_sems.at[0])
        take(one, send_sems.at[1])
        take(seven(n), send_sems.at[2])
        take(seven(n), send_sems.at[3])
        take(seven(n), send_sems.at[4])
        take(seven(n), send_sems.at[5])
        take(msend.at[:, pl.ds(0, n)], send_sems.at[6])
        take(one, send_sems.at[7])


    def sum_first(part):
        for k in range(PLANE):
            hloc[k] = part[4 * k : 4 * k + 4]
        on_plane(lambda d, pp: put(hloc.at[pp], h1.at[p], sum_send.at[0], sum_recv.at[0], plane_dev(pp)))
        h1[p] = hloc[p]

    def sum_second(par):
        take(h1.at[pl.ds(0, 7)], sum_recv.at[0])
        piece = jnp.sum(h1[...], axis=0)
        s2[...] = piece
        h2[par, m] = piece
        on_sheet(lambda dev: put(s2, h2.at[par, m], sum_send.at[1], sum_recv.at[1 + par], dev))

    def sum_third(par):
        take(h2.at[par, pl.ds(0, 31)], sum_recv.at[1 + par])
        h3[p] = jnp.sum(h2[par], axis=0)
        on_plane(lambda d, pp: put(h3.at[p], h3.at[p], sum_send.at[2], sum_recv.at[3], plane_dev(pp)))

    def sum_result():
        take(h1.at[pl.ds(0, 7)], sum_recv.at[3])
        h = jnp.concatenate([h3[k] for k in range(PLANE)], axis=0)
        h = h * (1.0 / (N_ROW * N_COL * WIDTH))
        return [h[:, k * K : (k + 1) * K] for k in range(3)]

    def sum_left(par):
        take(h1.at[pl.ds(0, 7)], sum_send.at[0])
        take(h2.at[par, pl.ds(0, 31)], sum_send.at[1])

    lane = lax.broadcasted_iota(jnp.int32, (K, 4 * K), 1)

    def split_in_three(value, start):
        for k in range(3):
            part = value.astype(BF16)
            split[k, start : start + K] = part
            value = value - part.astype(F32)

    split[...] = jnp.zeros_like(split)
    split_in_three(cur_ref[...], 0)
    split_in_three(prev_ref[...], K)

    xband[1, 1, :K] = cur_ref[...].astype(BF16)
    xband[1, 1, K:] = prev_ref[...].astype(BF16)
    q_and_p = ty[K:, :WIDTH]
    both = dot_nt(q_and_p, jnp.concatenate([q_and_p, ty[2 * K :, :WIDTH], ty[2 * K :, :WIDTH]], axis=0))
    pl.semaphore_wait(barrier, 7 + 31)
    spread(2 * K, 1)
    sum_first(jnp.where(lane < 2 * K, both[:K], both[K:]))
    own_forward(2 * K, 1)
    sum_second(1)
    pass_on(2 * K, 1)
    forward(2 * K, 1, 0)
    forward(2 * K, 1, 1)
    mirror_near(2 * K, 1)
    mirror_far(2 * K, 1)
    send_over(2 * K, 1)
    sum_third(1)
    images = image_whole(2 * K, 1, image_here(2 * K, 1, ty[K:, :WIDTH]))
    ty[K:, WIDTH:] = images
    xband[0, 1, :K] = images[:K].astype(BF16)
    ty[:K, :WIDTH] = xband[0, 1, :K].astype(F32)
    all_left(2 * K)
    for k, value in enumerate(sum_result()):
        known[1 + k] = value
    sum_left(1)
    take(h1.at[pl.ds(0, 7)], sum_send.at[2])

    def iteration(it, carry):
        par = lax.rem(it, 2)
        more = it < ITERS - 1

        image = xband[par, 1, :K]
        split[0, 2 * K : 3 * K] = image
        terms = [
            lax.dot_general(
                image, split[k], (((1,), (1,)), ((), ())), preferred_element_type=F32
            )
            for k in range(3)
        ]
        sum_first(terms[0] + terms[1] + terms[2])

        @pl.when(more)
        def _():
            spread(K, par)

        @pl.when(it > 0)
        def _():
            known[3] = known[1]
            known[1] = dot_nt(dot_nn(held[0], held[1]), held[0])
            known[2] = dot_nn(held[0], held[2])

        b, q_q, q_p, p_p = (known[k] for k in range(4))
        b_qp = dot_nt(b, q_p)
        b_pp = b - dot_nn(b, p_p)
        q_rest = q_q - dot_nt(q_p, q_p)
        p_rest = q_p - dot_nn(q_p, p_p)

        @pl.when(more)
        def _():
            own_forward(K, par)

        sum_second(par)

        @pl.when(more)
        def _():
            pass_on(K, par)
            forward(K, par, 0)
            forward(K, par, 1)
            mirror_near(K, par)

        sum_third(par)

        @pl.when(more)
        def _():
            mirror_far(K, par)
            send_over(K, par)
            ty[:K, WIDTH:] = image_here(K, par, ty[:K, :WIDTH])
            all_left(K)

        sum_left(par)
        im_q, im_p, im_im = sum_result()
        diag_t = im_q - b_qp
        back = im_p + b_pp
        cp = back - dot_nn(diag_t, q_p)
        t_q = im_q - dot_nt(back, q_p) - dot_nn(diag_t, q_rest)
        t_p = im_p - dot_nn(back, p_p) - dot_nn(diag_t, p_rest)
        gram = im_im - dot_nt(diag_t, im_q) - dot_nt(cp, im_p) - dot_nt(t_q, diag_t) - dot_nt(t_p, cp)
        rest = dot_nn(cp, ty[2 * K :]) + dot_nn(diag_t, ty[K : 2 * K])
        upper, inverse = factor(gram)

        @pl.when(more)
        def _():
            ty[:K, WIDTH:] = image_whole(K, par, ty[:K, WIDTH:])

        following = dot_nn(inverse, ty[:K] - rest)
        rounded = following[:, WIDTH:].astype(BF16)
        xband[1 - par, 1, :K] = rounded
        for k in range(3):
            split[k, K : 2 * K] = split[k, :K]
        split_in_three(following[:, :WIDTH], 0)
        ty[2 * K :] = ty[K : 2 * K]
        ty[K : 2 * K] = following
        ty[:K, :WIDTH] = rounded.astype(F32)
        diag_ref[it] = diag_t
        upper_ref[it] = upper
        known[0] = upper
        held[0] = inverse
        held[1] = gram
        held[2] = t_q
        take(h1.at[pl.ds(0, 7)], sum_send.at[2])
        return carry

    lax.fori_loop(0, ITERS, iteration, 0)
    out_ref[...] = ty[K : 2 * K, :WIDTH]


def lanczos(band, noise, previous, current, coupling):
    vmem = pl.BlockSpec(memory_space=pltpu.VMEM)
    panel = (K, WIDTH)
    two = (2 * K, WIDTH)
    piece = (4, 4 * K)
    return pl.pallas_call(
        lanczos_kernel,
        out_shape=(
            jax.ShapeDtypeStruct(panel, F32),
            jax.ShapeDtypeStruct((ITERS, K, K), F32),
            jax.ShapeDtypeStruct((ITERS, K, K), F32),
        ),
        in_specs=[vmem, vmem, vmem, vmem, vmem],
        out_specs=(vmem, vmem, vmem),
        scratch_shapes=[
            pltpu.VMEM((3 * K, 2 * WIDTH), F32),
            pltpu.VMEM((4, K, K), F32),
            pltpu.VMEM((3, K, K), F32),
            pltpu.VMEM((3, 4 * K, WIDTH), BF16),
            pltpu.VMEM((2, 3) + two, BF16),
            pltpu.VMEM((2, 2, PLANE) + two, BF16),
            pltpu.VMEM((N_COL,) + two, F32),
            pltpu.VMEM((2, 7) + two, BF16),
            pltpu.VMEM((2,) + two, F32),
            pltpu.VMEM((2, 2, 7) + two, BF16),
            pltpu.VMEM(two, BF16),
            pltpu.VMEM((2,) + two, BF16),
            pltpu.VMEM((2,) + two, BF16),
            pltpu.VMEM((2, 2) + two, BF16),
            pltpu.VMEM((2 * K, 3 * WIDTH), F32),
            pltpu.VMEM((8,) + piece, F32),
            pltpu.VMEM((8,) + piece, F32),
            pltpu.VMEM(piece, F32),
            pltpu.VMEM((2, 32) + piece, F32),
            pltpu.VMEM((8,) + piece, F32),
            pltpu.SemaphoreType.DMA((8,)),
            pltpu.SemaphoreType.DMA((2, 8)),
            pltpu.SemaphoreType.DMA((3,)),
            pltpu.SemaphoreType.DMA((4,)),
        ],
        compiler_params=pltpu.CompilerParams(
            collective_id=0, has_side_effects=True, vmem_limit_bytes=40 * 2**20
        ),
        name="lanczos",
    )(band, noise, previous, current, coupling)


def on_device(
    kernel_tiles, tile_rows, tile_cols, tile_counts, noise, prev_block, current_block, prev_coupling
):
    band = build_band(kernel_tiles[0, 0], tile_rows[0], tile_cols[0], tile_counts)
    following, diag_t, upper = lanczos(band, noise[None, :], prev_block, current_block, prev_coupling)
    return (following, jnp.swapaxes(diag_t, 1, 2), jnp.swapaxes(upper, 1, 2))


def solution(mesh):
    in_specs = (
        P("row", "col", None, None, None),
        P("row", "col", None),
        P("row", "col", None),
        P("row", "col"),
        P(("row", "col")),
        P(None, ("row", "col")),
        P(None, ("row", "col")),
        P(),
    )
    out_specs = (P(None, ("row", "col")), P(), P())
    return jax.shard_map(
        on_device, mesh=mesh, in_specs=in_specs, out_specs=out_specs, check_vma=False
    )
```
